32 devices in a mesh: row: 8 (over z, core), col: 4 (over y, x).
Axes of the slice: x: 2, y: 2, z: 4, core: 2. Of those that a mesh axis runs over, the one named last changes fastest.
Arguments:
- a_tiles: bfloat16 [8, 4, 2, 16, 128, 128], P('row', 'col'), may hold values from 0 to 0.25
- a_index: int32 [8, 4, 2, 16], P('row', 'col'), may hold values from 0 to 127, as said below
- a_count: int32 [8, 4, 2], P('row', 'col'), may hold values from 1 to 16
- b_tiles: bfloat16 [8, 4, 16, 128, 128], P('row', 'col'), may hold values from 0 to 0.25
- b_index: int32 [8, 4, 16], P('row', 'col'), may hold values from 0 to 127, as said below
- b_count: int32 [8, 4], P('row', 'col'), may hold values from 1 to 16
- c_partial: float32 [4096, 2048], P('row', 'col'), may hold values from 0.25 to 60, as said below
- prune_mask: int32 [32, 16], P('row', 'col'), may hold values from 0 to 1, as said below
Outputs:
- renormed: float32 [4096, 2048], P('row', 'col')
The draws below stay inside these ranges and needn't reach their ends.
Inputs may be any that keep to these rules, and one draw needn't show every extreme that they name: `a_index`: within one device and section the slots are distinct. `b_index`: within one device the slots are distinct. `prune_mask`: every block column keeps at least one tile. `c_partial`: positive entries.
All inputs are finite; a program needn't handle non-finite values.
Results may differ from the reference program's by a relative error of at most 0.0003.
Values may be sent and summed in bfloat16 or wider, within the bound.
A program may use at most 64 MiB of HBM per device.

```python
import jax
import jax.numpy as jnp
from jax import lax

TILE = 128
MB = 4
NB = 4
W = 32
KA = 16
KB = 16
SECTIONS = 2
ROWS = 4096
COLS = 2048
RB = 32
CB = 16
N_ROW = 8
N_COL = 4


def draw_a_index(key, part):
    key = jax.random.fold_in(key, 11)
    keys = jax.random.split(key, N_ROW * N_COL * SECTIONS)
    picks = jax.vmap(lambda k: jax.random.permutation(k, MB * W)[:KA])(keys)
    return picks.reshape(N_ROW, N_COL, SECTIONS, KA).astype(jnp.int32)


def draw_a_count(key, part):
    key = jax.random.fold_in(key, 12)
    counts = jax.random.randint(key, (N_ROW, N_COL, SECTIONS), 1, KA + 1)
    counts = counts.at[0, N_COL - 1, 0].set(KA)
    counts = counts.at[N_ROW - 1, N_COL - 1, 1].set(1)
    return counts.astype(jnp.int32)


def draw_b_index(key, part):
    key = jax.random.fold_in(key, 13)
    keys = jax.random.split(key, N_ROW * N_COL)
    picks = jax.vmap(lambda k: jax.random.permutation(k, W * NB)[:KB])(keys)
    return picks.reshape(N_ROW, N_COL, KB).astype(jnp.int32)


def draw_b_count(key, part):
    key = jax.random.fold_in(key, 14)
    counts = jax.random.randint(key, (N_ROW, N_COL), 1, KB + 1)
    counts = counts.at[N_ROW - 2, 0].set(KB)
    counts = counts.at[N_ROW - 1, N_COL - 1].set(1)
    return counts.astype(jnp.int32)


def draw_prune_mask(key, part):
    key = jax.random.fold_in(key, 15)
    coins = jax.random.randint(key, (RB, CB), 0, 2)
    forced = (jnp.arange(RB)[:, None] == jnp.arange(CB)[None, :]).astype(jnp.int32)
    return jnp.maximum(coins, forced).astype(jnp.int32)


def draw_c_partial(key, part):
    key = jax.random.fold_in(key, 16)
    first = jax.random.fold_in(key, 0)
    rising = 1.0 + 2.0 * jnp.arange(ROWS, dtype=jnp.float32) / (ROWS - 1)
    base = jax.random.uniform(first, (ROWS, COLS), jnp.float32, 0.5, 1.5)
    return (base * rising[:, None]).astype(jnp.float32)


def level_of(rng, dims, pieces, least, largest):
    level = 1.0
    for dim, blocks in pieces:
        heights = jax.random.uniform(jax.random.fold_in(jax.random.fold_in(rng, 6), dim), (blocks,), jnp.float32, least / len(pieces), largest / len(pieces))
        level = level * jnp.repeat(jnp.exp(heights), dims[dim] // blocks).reshape((-1,) + (1,) * (len(dims) - 1 - dim))
    return level


def setup_inputs(seed: int = 0) -> dict:
    arg_keys = jax.random.split(jax.random.key(seed), 9)
    return {
        "a_tiles": jnp.clip(0.25 * jax.random.uniform(arg_keys[0], (N_ROW, N_COL, SECTIONS, KA, TILE, TILE), jnp.float32) ** level_of(arg_keys[0], (N_ROW, N_COL, SECTIONS, KA, TILE, TILE), ((0, 8), (1, 4)), -0.2, 0.2), 0.0, 0.25).astype(jnp.bfloat16),
        "a_index": draw_a_index(jax.random.fold_in(arg_keys[8], 71), 0),
        "a_count": draw_a_count(jax.random.fold_in(arg_keys[8], 71), 0),
        "b_tiles": jnp.clip(0.25 * jax.random.uniform(arg_keys[3], (N_ROW, N_COL, KB, TILE, TILE), jnp.float32) ** level_of(arg_keys[3], (N_ROW, N_COL, KB, TILE, TILE), ((0, 8), (1, 4)), -0.2, 0.2), 0.0, 0.25).astype(jnp.bfloat16),
        "b_index": draw_b_index(jax.random.fold_in(arg_keys[8], 71), 0),
        "b_count": draw_b_count(jax.random.fold_in(arg_keys[8], 71), 0),
        "c_partial": draw_c_partial(jax.random.fold_in(arg_keys[8], 71), 0),
        "prune_mask": draw_prune_mask(jax.random.fold_in(arg_keys[8], 71), 0),
    }


def left_panel(tiles, index, count):
    live = (jnp.arange(KA) < count[:, None]).astype(jnp.float32)
    onehot = (index[:, :, None] == jnp.arange(MB * W)[None, None, :]).astype(jnp.float32) * live[:, :, None]
    dense = jnp.einsum('rap,rauv->rpuv', onehot, tiles.astype(jnp.float32), precision=lax.Precision.HIGHEST)
    dense = dense.reshape(N_ROW, MB, W, TILE, TILE).transpose(0, 1, 3, 2, 4)
    return dense.reshape(ROWS, W * TILE)


def right_panel(tiles, index, count):
    live = (jnp.arange(KB) < count[:, None]).astype(jnp.float32)
    onehot = (index[:, :, None] == jnp.arange(W * NB)[None, None, :]).astype(jnp.float32) * live[:, :, None]
    dense = jnp.einsum('cbp,cbuv->cpuv', onehot, tiles.astype(jnp.float32), precision=lax.Precision.HIGHEST)
    dense = dense.reshape(N_COL, W, NB, TILE, TILE).transpose(1, 3, 0, 2, 4)
    return dense.reshape(W * TILE, COLS)


def reference(a_tiles, a_index, a_count, b_tiles, b_index, b_count, c_partial, prune_mask):
    expanded = c_partial
    for section in range(SECTIONS):
        left = left_panel(a_tiles[:, N_COL - 1, section], a_index[:, N_COL - 1, section], a_count[:, N_COL - 1, section])
        right = right_panel(b_tiles[N_ROW - 2 + section], b_index[N_ROW - 2 + section], b_count[N_ROW - 2 + section])
        expanded = expanded + jnp.dot(left, right, precision=lax.Precision.HIGHEST)
    keep = jnp.repeat(jnp.repeat(prune_mask.astype(jnp.float32), TILE, axis=0), TILE, axis=1)
    kept = expanded * expanded * keep
    colsum = jnp.sum(kept, axis=0)
    return kept * (ROWS / colsum)[None, :]
```

```python
import functools

import jax
import jax.numpy as jnp
from jax import lax
from jax.experimental import pallas as pl
from jax.experimental.pallas import tpu as pltpu
from jax.sharding import PartitionSpec as P

MB = 4
NB = 4
W = 32
KA = 16
KB = 16
SECTIONS = 2
TILE = 128
STEP = 2
PARTS = KA // 2 // STEP
MESH = pl.DeviceIdType.MESH


def grid_of(n_col):
    nx = max(d for d in range(1, n_col + 1) if n_col % d == 0 and d * d <= n_col)
    return n_col // nx, nx


def snake(index, outer, inner):
    o, i = index // inner, index % inner
    return o, (1 - o % 2) * i + (o % 2) * (inner - 1 - i)


def path_position(col, path, ny, nx):
    y, x = ny - 1 - col // nx, nx - 1 - col % nx
    if path == 0:
        return y * nx + (1 - y % 2) * x + (y % 2) * (nx - 1 - x)
    return x * ny + (1 - x % 2) * y + (x % 2) * (ny - 1 - y)


def path_column(position, path, ny, nx):
    if path == 0:
        y, x = snake(position, ny, nx)
    else:
        x, y = snake(position, nx, ny)
    return (ny - 1 - y) * nx + (nx - 1 - x)


def kernel(
    n_row, n_col, ai_ref, ac_ref, bi_ref, bc_ref, mask_ref, a_hbm, b_hbm, c_hbm,
    kept_hbm, scale_ref,
    lt0, lt1, rt0, rt1, ma, mb, table, table_smem, acc, sums,
    a_send, a_recv, b_send, b_recv, sib_send, sib_recv, ma_send, ma_recv, mb_send, mb_recv,
    cs_send, cs_recv, loc,
):
    row = lax.axis_index("row")
    col = lax.axis_index("col")
    pair, core = row // 2, row % 2
    last_pair = n_row // 2 - 1
    ny, nx = grid_of(n_col)
    lts, rts = (lt0, lt1), (rt0, rt1)
    total_rows = n_row * MB * TILE

    load_c = pltpu.make_async_copy(c_hbm, acc, loc.at[0])
    load_c.start()

    barrier = pltpu.get_barrier_semaphore()
    for d in range(1, n_row):
        pl.semaphore_signal(barrier, inc=1, device_id=((row + d) % n_row, col), device_id_type=MESH)
    for d in range(1, n_col):
        pl.semaphore_signal(barrier, inc=1, device_id=(row, (col + d) % n_col), device_id_type=MESH)

    lane = lax.broadcasted_iota(jnp.int32, (1, TILE), 1)

    @pl.when(col == n_col - 1)
    def _():
        for s in range(SECTIONS):
            count = ac_ref[0, 0, s]
            target = jnp.full((1, TILE), -2, jnp.int32)
            place = jnp.full((1, TILE), KA, jnp.int32)
            for a in range(KA):
                slot = ai_ref[0, 0, s, a]
                live = a < count
                inner = jnp.where(live, (slot % W) * NB, -64)
                block = jnp.where(live, slot // W, -1)
                target = jnp.where(lane // NB == a, inner + lane % NB, target)
                place = jnp.where(lane == block * KA + a, jnp.where(live, a, KA), place)
            ma[s : s + 1, :] = target
            ma[SECTIONS + s : SECTIONS + s + 1, :] = place

    for s in range(SECTIONS):

        @pl.when(row == n_row - SECTIONS + s)
        def _(s=s):
            count = bc_ref[0, 0]
            for b in range(KB):
                slot = jnp.where(b < count, bi_ref[0, 0, b], -1)
                mb[s, b : b + 1, :] = jnp.full((1, TILE), slot, jnp.int32)

    for s in range(SECTIONS):
        lts[s][KA] = jnp.zeros((TILE, TILE), jnp.bfloat16)
        rts[s][KB] = jnp.zeros((TILE, TILE), jnp.bfloat16)

    pl.semaphore_wait(barrier, n_row - 1 + n_col - 1)

    positions = [path_position(col, p, ny, nx) for p in range(2)]
    is_left_root = col == n_col - 1

    def next_col(p):
        return path_column((positions[p] + 1) % n_col, p, ny, nx)

    def a_copy(p, i, from_hbm):
        s, c = i // PARTS, i % PARTS
        tiles = pl.ds(p * (KA // 2) + c * STEP, STEP)
        return pltpu.make_async_remote_copy(
            src_ref=a_hbm.at[0, 0, s, tiles] if from_hbm else lts[s].at[tiles],
            dst_ref=lts[s].at[tiles],
            send_sem=a_send.at[p, i], recv_sem=a_recv.at[p, i],
            device_id=(row, next_col(p)), device_id_type=MESH,
        )

    def ma_copy():
        return pltpu.make_async_remote_copy(
            src_ref=ma, dst_ref=ma, send_sem=ma_send.at[0], recv_sem=ma_recv.at[0],
            device_id=(row, next_col(0)), device_id_type=MESH,
        )

    def a_local(s):
        return pltpu.make_async_copy(a_hbm.at[0, 0, s], lts[s].at[pl.ds(0, KA)], loc.at[1 + s])

    below = (pair - 1 + last_pair + 1) % (last_pair + 1)
    sibling = pair * 2 + 1 - core

    def b_root_copy(s, k, c):
        tiles = pl.ds(k * (KB // 2) + c * STEP, STEP)
        return pltpu.make_async_remote_copy(
            src_ref=b_hbm.at[0, 0, tiles], dst_ref=rts[s].at[tiles],
            send_sem=b_send.at[k * PARTS + c], recv_sem=b_recv.at[s * PARTS + c],
            device_id=(below * 2 + k, col), device_id_type=MESH,
        )

    def b_root_sibling(s):
        return pltpu.make_async_remote_copy(
            src_ref=b_hbm.at[0, 0], dst_ref=rts[s].at[pl.ds(0, KB)],
            send_sem=sib_send.at[0], recv_sem=sib_recv.at[s * PARTS],
            device_id=(sibling, col), device_id_type=MESH,
        )

    def mb_copy(s, target, sem):
        return pltpu.make_async_remote_copy(
            src_ref=mb.at[s], dst_ref=mb.at[s], send_sem=mb_send.at[sem], recv_sem=mb_recv.at[s],
            device_id=(target, col), device_id_type=MESH,
        )

    def b_tiles(i, k):
        return pl.ds(k * (KB // 2) + (i % PARTS) * STEP, STEP)

    def b_copy(i):
        ref = rts[i // PARTS].at[b_tiles(i, core)]
        return pltpu.make_async_remote_copy(
            src_ref=ref, dst_ref=ref, send_sem=b_send.at[i], recv_sem=b_recv.at[i],
            device_id=(below * 2 + core, col), device_id_type=MESH,
        )

    def sib_copy(i):
        ref = rts[i // PARTS].at[b_tiles(i, core)]
        return pltpu.make_async_remote_copy(
            src_ref=ref, dst_ref=ref, send_sem=sib_send.at[i], recv_sem=sib_recv.at[i],
            device_id=(sibling, col), device_id_type=MESH,
        )

    def sib_arrival(i):
        ref = rts[i // PARTS].at[b_tiles(i, 1 - core)]
        return pltpu.make_async_remote_copy(
            src_ref=ref, dst_ref=ref, send_sem=sib_send.at[i], recv_sem=sib_recv.at[i],
            device_id=(sibling, col), device_id_type=MESH,
        )

    def b_local(s):
        return pltpu.make_async_copy(b_hbm.at[0, 0], rts[s].at[pl.ds(0, KB)], loc.at[3])

    steps = SECTIONS * PARTS
    in_chain = pair < last_pair

    @pl.when(is_left_root)
    def _():
        ma_copy().start()
        for i in range(steps):
            for p in range(2):
                a_copy(p, i, True).start()
        for s in range(SECTIONS):
            a_local(s).start()

    for s in range(SECTIONS):

        @pl.when(row == n_row - SECTIONS + s)
        def _(s=s):
            for k in range(2):
                mb_copy(s, below * 2 + k, k).start()
            mb_copy(s, sibling, 2).start()
            for c in range(PARTS):
                for k in range(2):
                    b_root_copy(s, k, c).start()
            b_root_sibling(s).start()
            b_local(s).start()

    @pl.when(positions[0] > 0)
    def _():
        ma_copy().wait_recv()

        @pl.when(positions[0] < n_col - 1)
        def _():
            ma_copy().start()

    def forward(i):
        for p in range(2):

            @pl.when(positions[p] > 0)
            def _(p=p):
                a_copy(p, i, False).wait_recv()

                @pl.when(positions[p] < n_col - 1)
                def _():
                    a_copy(p, i, False).start()

        @pl.when(in_chain)
        def _():
            b_copy(i).wait_recv()

            @pl.when(pair > 0)
            def _():
                b_copy(i).start()

            sib_copy(i).start()

    def section_ready(s):
        @pl.when(is_left_root)
        def _():
            a_local(s).wait()

        @pl.when(in_chain)
        def _():
            for c in range(PARTS):
                sib_arrival(s * PARTS + c).wait_recv()

        @pl.when(row == n_row - SECTIONS + s)
        def _():
            b_local(s).wait()

        @pl.when(row == n_row - 1 - s)
        def _():
            b_root_sibling(s).wait_recv()

    for s in range(SECTIONS):

        @pl.when(in_chain)
        def _(s=s):
            mb_copy(s, below * 2 + core, s).wait_recv()

            @pl.when(pair > 0)
            def _():
                mb_copy(s, below * 2 + core, s).start()

        @pl.when(row == n_row - 1 - s)
        def _(s=s):
            mb_copy(s, sibling, s).wait_recv()

    row_id = lax.broadcasted_iota(jnp.int32, (KB, TILE), 0)
    for s in range(SECTIONS):
        hit = mb[s] == ma[s : s + 1, :]
        table[s : s + 1, :] = jnp.min(jnp.where(hit, row_id, KB), axis=0, keepdims=True)
    table[SECTIONS : 2 * SECTIONS, :] = ma[SECTIONS : 2 * SECTIONS, :]
    to_smem = pltpu.make_async_copy(table, table_smem, loc.at[4])
    to_smem.start()

    group = KA // PARTS

    def product(s, j):
        left = jnp.concatenate(
            [
                jnp.concatenate(
                    [lts[s][table_smem[SECTIONS + s, m * KA + j * group + a]] for a in range(group)],
                    axis=1,
                )
                for m in range(MB)
            ],
            axis=0,
        )
        right = jnp.concatenate(
            [
                jnp.concatenate(
                    [rts[s][table_smem[s, (j * group + a) * NB + n]] for n in range(NB)], axis=1
                )
                for a in range(group)
            ],
            axis=0,
        )
        acc[...] += jnp.dot(left, right, preferred_element_type=jnp.float32)

    for i in range(PARTS):
        forward(i)
    to_smem.wait()
    load_c.wait()
    for s in range(SECTIONS):
        section_ready(s)
        for j in range(PARTS):
            if s + 1 < SECTIONS:
                forward((s + 1) * PARTS + j)
            product(s, j)

    partial = jnp.zeros((1, NB * TILE), jnp.float32)
    for m in range(MB):
        keep = jnp.concatenate(
            [
                jnp.full((1, TILE), mask_ref[m, n].astype(jnp.float32), jnp.float32)
                for n in range(NB)
            ],
            axis=1,
        )
        block = acc[m * TILE : (m + 1) * TILE, :]
        kept = block * block * keep
        acc[m * TILE : (m + 1) * TILE, :] = kept
        partial = partial + jnp.sum(kept, axis=0, keepdims=True)
    store = pltpu.make_async_copy(acc, kept_hbm, loc.at[0])
    store.start()

    sums[row] = partial

    def cs_copy(target, slot):
        return pltpu.make_async_remote_copy(
            src_ref=sums.at[slot], dst_ref=sums.at[slot],
            send_sem=cs_send.at[target], recv_sem=cs_recv.at[slot],
            device_id=(target, col), device_id_type=MESH,
        )

    for d in range(1, n_row):
        cs_copy((row + d) % n_row, row).start()
    for d in range(1, n_row):
        source = (row + d) % n_row
        cs_copy(source, source).wait_recv()
    scale_ref[...] = total_rows / jnp.sum(sums[...], axis=0)

    for d in range(1, n_row):
        cs_copy((row + d) % n_row, row).wait_send()
    for p in range(2):

        @pl.when(positions[p] < n_col - 1)
        def _(p=p):
            for i in range(steps):
                a_copy(p, i, False).wait_send()

    @pl.when(positions[0] < n_col - 1)
    def _():
        ma_copy().wait_send()

    @pl.when(in_chain)
    def _():
        for i in range(steps):
            sib_copy(i).wait_send()

        @pl.when(pair > 0)
        def _():
            for i in range(steps):
                b_copy(i).wait_send()
            for s in range(SECTIONS):
                mb_copy(s, below * 2 + core, s).wait_send()

    for s in range(SECTIONS):

        @pl.when(row == n_row - SECTIONS + s)
        def _(s=s):
            for k in range(2):
                mb_copy(s, below * 2 + k, k).wait_send()
            mb_copy(s, sibling, 2).wait_send()
            for c in range(PARTS):
                for k in range(2):
                    b_root_copy(s, k, c).wait_send()
            b_root_sibling(s).wait_send()

    store.wait()


def local(n_row, n_col, a_tiles, a_index, a_count, b_tiles, b_index, b_count, c_partial, prune_mask):
    smem = pl.BlockSpec(memory_space=pltpu.SMEM)
    hbm = pl.BlockSpec(memory_space=pl.ANY)
    steps = SECTIONS * PARTS
    dma = pltpu.SemaphoreType.DMA
    rows, columns = c_partial.shape
    kept, scale = pl.pallas_call(
        functools.partial(kernel, n_row, n_col),
        out_shape=(
            jax.ShapeDtypeStruct((rows, columns), jnp.float32),
            jax.ShapeDtypeStruct((1, columns), jnp.float32),
        ),
        in_specs=[smem] * 5 + [hbm] * 3,
        out_specs=(hbm, pl.BlockSpec(memory_space=pltpu.VMEM)),
        scratch_shapes=[
            pltpu.VMEM((KA + 1, TILE, TILE), jnp.bfloat16),
            pltpu.VMEM((KA + 1, TILE, TILE), jnp.bfloat16),
            pltpu.VMEM((KB + 1, TILE, TILE), jnp.bfloat16),
            pltpu.VMEM((KB + 1, TILE, TILE), jnp.bfloat16),
            pltpu.VMEM((2 * SECTIONS, TILE), jnp.int32),
            pltpu.VMEM((SECTIONS, KB, TILE), jnp.int32),
            pltpu.VMEM((2 * SECTIONS, TILE), jnp.int32),
            pltpu.SMEM((2 * SECTIONS, TILE), jnp.int32),
            pltpu.VMEM((rows, columns), jnp.float32),
            pltpu.VMEM((n_row, 1, columns), jnp.float32),
            dma((2, steps)), dma((2, steps)),
            dma((steps,)), dma((steps,)), dma((steps,)), dma((steps,)),
            dma((1,)), dma((1,)), dma((3,)), dma((SECTIONS,)),
            dma((n_row,)), dma((n_row,)), dma((5,)),
        ],
        compiler_params=pltpu.CompilerParams(
            collective_id=0, has_side_effects=True, vmem_limit_bytes=32 * 1024 * 1024
        ),
        cost_estimate=pl.CostEstimate(
            flops=SECTIONS * 2 * rows * KA * TILE * columns, bytes_accessed=8 * rows * columns, transcendentals=0
        ),
    )(a_index, a_count, b_index, b_count, prune_mask, a_tiles, b_tiles, c_partial)
    return kept * scale


def solution(mesh):
    n_row, n_col = mesh.shape["row"], mesh.shape["col"]
    return jax.shard_map(
        functools.partial(local, n_row, n_col),
        mesh=mesh,
        in_specs=(
            P("row", "col", None, None, None, None),
            P("row", "col", None, None),
            P("row", "col", None),
            P("row", "col", None, None, None),
            P("row", "col", None),
            P("row", "col"),
            P("row", "col"),
            P("row", "col"),
        ),
        out_specs=P("row", "col"),
        check_vma=False,
    )
```

```python
import functools

import jax
import jax.numpy as jnp
from jax import lax
from jax.experimental import pallas as pl
from jax.experimental.pallas import tpu as pltpu
from jax.sharding import PartitionSpec as P

MB = 4
NB = 4
W = 32
KA = 16
KB = 16
SECTIONS = 2
TILE = 128
STEP = 2
PARTS = KA // 2 // STEP
MESH = pl.DeviceIdType.MESH


def grid_of(n_col):
    nx = max(d for d in range(1, n_col + 1) if n_col % d == 0 and d * d <= n_col)
    return n_col // nx, nx


def snake(index, outer, inner):
    o, i = index // inner, index % inner
    return o, (1 - o % 2) * i + (o % 2) * (inner - 1 - i)


def path_position(col, path, ny, nx):
    y, x = ny - 1 - col // nx, nx - 1 - col % nx
    if path == 0:
        return y * nx + (1 - y % 2) * x + (y % 2) * (nx - 1 - x)
    return x * ny + (1 - x % 2) * y + (x % 2) * (ny - 1 - y)


def path_column(position, path, ny, nx):
    if path == 0:
        y, x = snake(position, ny, nx)
    else:
        x, y = snake(position, nx, ny)
    return (ny - 1 - y) * nx + (nx - 1 - x)


def kernel(
    n_row, n_col, ai_hbm, ac_hbm, bi_hbm, bc_hbm, mask_hbm, a_hbm, b_hbm, c_hbm,
    kept_hbm, scale_ref,
    ai_ref, ac_ref, bi_ref, bc_ref, mask_ref, lt0, lt1, rt0, rt1, ma, mb, table, table_smem, acc, sums,
    a_send, a_recv, b_send, b_recv, sib_send, sib_recv, ma_send, ma_recv, mb_send, mb_recv,
    cs_send, cs_recv, loc,
):
    row = lax.axis_index("row")
    col = lax.axis_index("col")
    pair, core = row // 2, row % 2
    last_pair = n_row // 2 - 1
    ny, nx = grid_of(n_col)
    lts, rts = (lt0, lt1), (rt0, rt1)
    total_rows = n_row * MB * TILE

    load_c = pltpu.make_async_copy(c_hbm, acc, loc.at[0])
    load_c.start()
    small = [
        pltpu.make_async_copy(source, target, loc.at[5 + i])
        for i, (source, target) in enumerate(
            ((ai_hbm, ai_ref), (ac_hbm, ac_ref), (bi_hbm, bi_ref), (bc_hbm, bc_ref), (mask_hbm, mask_ref))
        )
    ]
    for copy in small:
        copy.start()

    barrier = pltpu.get_barrier_semaphore()
    for d in range(1, n_row):
        pl.semaphore_signal(barrier, inc=1, device_id=((row + d) % n_row, col), device_id_type=MESH)
    for d in range(1, n_col):
        pl.semaphore_signal(barrier, inc=1, device_id=(row, (col + d) % n_col), device_id_type=MESH)

    for s in range(SECTIONS):
        lts[s][KA] = jnp.zeros((TILE, TILE), jnp.bfloat16)
        rts[s][KB] = jnp.zeros((TILE, TILE), jnp.bfloat16)

    for copy in small:
        copy.wait()
    lane = lax.broadcasted_iota(jnp.int32, (1, TILE), 1)

    @pl.when(col == n_col - 1)
    def _():
        for s in range(SECTIONS):
            count = ac_ref[0, 0, s]
            target = jnp.full((1, TILE), -2, jnp.int32)
            place = jnp.full((1, TILE), KA, jnp.int32)
            for a in range(KA):
                slot = ai_ref[0, 0, s, a]
                live = a < count
                inner = jnp.where(live, (slot % W) * NB, -64)
                block = jnp.where(live, slot // W, -1)
                target = jnp.where(lane // NB == a, inner + lane % NB, target)
                place = jnp.where(lane == block * KA + a, jnp.where(live, a, KA), place)
            ma[s : s + 1, :] = target
            ma[SECTIONS + s : SECTIONS + s + 1, :] = place

    for s in range(SECTIONS):

        @pl.when(row == n_row - SECTIONS + s)
        def _(s=s):
            count = bc_ref[0, 0]
            for b in range(KB):
                slot = jnp.where(b < count, bi_ref[0, 0, b], -1)
                mb[s, b : b + 1, :] = jnp.full((1, TILE), slot, jnp.int32)

    pl.semaphore_wait(barrier, n_row - 1 + n_col - 1)

    positions = [path_position(col, p, ny, nx) for p in range(2)]
    is_left_root = col == n_col - 1

    def next_col(p):
        return path_column((positions[p] + 1) % n_col, p, ny, nx)

    def a_copy(p, s, c, from_hbm):
        i = s * PARTS + c
        tiles = pl.ds(p * (KA // 2) + c * STEP, STEP)
        return pltpu.make_async_remote_copy(
            src_ref=a_hbm.at[0, 0, s, tiles] if from_hbm else lts[s].at[tiles],
            dst_ref=lts[s].at[tiles],
            send_sem=a_send.at[p, i], recv_sem=a_recv.at[p, i],
            device_id=(row, next_col(p)), device_id_type=MESH,
        )

    def ma_copy():
        return pltpu.make_async_remote_copy(
            src_ref=ma, dst_ref=ma, send_sem=ma_send.at[0], recv_sem=ma_recv.at[0],
            device_id=(row, next_col(0)), device_id_type=MESH,
        )

    def a_local(s):
        return pltpu.make_async_copy(a_hbm.at[0, 0, s], lts[s].at[pl.ds(0, KA)], loc.at[1 + s])

    below = (pair - 1 + last_pair + 1) % (last_pair + 1)
    sibling = pair * 2 + 1 - core

    def b_root_copy(s, k, c):
        tiles = pl.ds(k * (KB // 2) + c * STEP, STEP)
        return pltpu.make_async_remote_copy(
            src_ref=b_hbm.at[0, 0, tiles], dst_ref=rts[s].at[tiles],
            send_sem=b_send.at[k * PARTS + c], recv_sem=b_recv.at[s * PARTS + c],
            device_id=(below * 2 + k, col), device_id_type=MESH,
        )

    def b_root_sibling(s):
        return pltpu.make_async_remote_copy(
            src_ref=b_hbm.at[0, 0], dst_ref=rts[s].at[pl.ds(0, KB)],
            send_sem=sib_send.at[0], recv_sem=sib_recv.at[s * PARTS],
            device_id=(sibling, col), device_id_type=MESH,
        )

    def mb_copy(s, target, sem):
        return pltpu.make_async_remote_copy(
            src_ref=mb.at[s], dst_ref=mb.at[s], send_sem=mb_send.at[sem], recv_sem=mb_recv.at[s],
            device_id=(target, col), device_id_type=MESH,
        )

    def b_chain_copy(s, c, k, target, send, recv):
        ref = rts[s].at[pl.ds(k * (KB // 2) + c * STEP, STEP)]
        i = s * PARTS + c
        return pltpu.make_async_remote_copy(
            src_ref=ref, dst_ref=ref, send_sem=send.at[i], recv_sem=recv.at[i],
            device_id=(target, col), device_id_type=MESH,
        )

    def b_copy(s, c):
        return b_chain_copy(s, c, core, below * 2 + core, b_send, b_recv)

    def sib_copy(s, c):
        return b_chain_copy(s, c, core, sibling, sib_send, sib_recv)

    def sib_arrival(s, c):
        return b_chain_copy(s, c, 1 - core, sibling, sib_send, sib_recv)

    def b_local(s):
        return pltpu.make_async_copy(b_hbm.at[0, 0], rts[s].at[pl.ds(0, KB)], loc.at[3])

    steps = SECTIONS * PARTS
    in_chain = pair < last_pair

    @pl.when(is_left_root)
    def _():
        ma_copy().start()
        for i in range(steps):
            for p in range(2):
                a_copy(p, i // PARTS, i % PARTS, True).start()
        for s in range(SECTIONS):
            a_local(s).start()

    for s in range(SECTIONS):

        @pl.when(row == n_row - SECTIONS + s)
        def _(s=s):
            for k in range(2):
                mb_copy(s, below * 2 + k, k).start()
            mb_copy(s, sibling, 2).start()
            for c in range(PARTS):
                for k in range(2):
                    b_root_copy(s, k, c).start()
            b_root_sibling(s).start()
            b_local(s).start()

    def forward(t):
        for p in range(2):
            i = t - (positions[p] - 1)
            passes = (positions[p] > 0) & (positions[p] < n_col - 1)
            if p == 0:

                @pl.when(passes & (i == 0))
                def _():
                    ma_copy().wait_recv()
                    ma_copy().start()

            for s in range(SECTIONS):
                c = i - s * PARTS

                @pl.when(passes & (c >= 0) & (c < PARTS))
                def _(p=p, s=s, c=c):
                    a_copy(p, s, c, False).wait_recv()
                    a_copy(p, s, c, False).start()

        i = t - (last_pair - 1 - pair)
        for s in range(SECTIONS):
            c = i - s * PARTS

            @pl.when(in_chain & (c == 0))
            def _(s=s):
                mb_copy(s, below * 2 + core, s).wait_recv()

                @pl.when(pair > 0)
                def _():
                    mb_copy(s, below * 2 + core, s).start()

            @pl.when(in_chain & (c >= 0) & (c < PARTS))
            def _(s=s, c=c):
                b_copy(s, c).wait_recv()

                @pl.when(pair > 0)
                def _():
                    b_copy(s, c).start()

                sib_copy(s, c).start()

    def section_ready(s):
        for p in range(2):

            @pl.when(positions[p] == n_col - 1)
            def _(p=p):
                for c in range(PARTS):
                    a_copy(p, s, c, False).wait_recv()

        @pl.when(is_left_root)
        def _():
            a_local(s).wait()

        @pl.when(in_chain)
        def _():
            for c in range(PARTS):
                sib_arrival(s, c).wait_recv()

        @pl.when(row == n_row - SECTIONS + s)
        def _():
            b_local(s).wait()

        @pl.when(row == n_row - 1 - s)
        def _():
            b_root_sibling(s).wait_recv()

    most = max(n_col - 3, last_pair - 1, 0)
    for t in range(PARTS + most):
        forward(t)

    @pl.when(positions[0] == n_col - 1)
    def _():
        ma_copy().wait_recv()

    for s in range(SECTIONS):
        @pl.when(row == n_row - 1 - s)
        def _(s=s):
            mb_copy(s, sibling, s).wait_recv()

    group = KA // PARTS

    def product(s, j):
        left = jnp.concatenate(
            [
                jnp.concatenate(
                    [lts[s][table_smem[s, 1, m * KA + j * group + a]] for a in range(group)],
                    axis=1,
                )
                for m in range(MB)
            ],
            axis=0,
        )
        right = jnp.concatenate(
            [
                jnp.concatenate(
                    [rts[s][table_smem[s, 0, (j * group + a) * NB + n]] for n in range(NB)], axis=1
                )
                for a in range(group)
            ],
            axis=0,
        )
        acc[...] += jnp.dot(left, right, preferred_element_type=jnp.float32)

    row_id = lax.broadcasted_iota(jnp.int32, (KB, TILE), 0)

    def make_table(s):
        table[0:1, :] = jnp.min(jnp.where(mb[s] == ma[s : s + 1, :], row_id, KB), axis=0, keepdims=True)
        table[1:2, :] = ma[SECTIONS + s : SECTIONS + s + 1, :]
        to_smem = pltpu.make_async_copy(table, table_smem.at[s], loc.at[4])
        to_smem.start()
        to_smem.wait()

    load_c.wait()
    for s in range(SECTIONS):
        section_ready(s)
        make_table(s)
        for j in range(PARTS):
            if s + 1 < SECTIONS:
                forward(PARTS + most + j)
            product(s, j)

    partial = jnp.zeros((1, NB * TILE), jnp.float32)
    for m in range(MB):
        keep = jnp.concatenate(
            [
                jnp.full((1, TILE), mask_ref[m, n].astype(jnp.float32), jnp.float32)
                for n in range(NB)
            ],
            axis=1,
        )
        block = acc[m * TILE : (m + 1) * TILE, :]
        kept = block * block * keep
        acc[m * TILE : (m + 1) * TILE, :] = kept
        partial = partial + jnp.sum(kept, axis=0, keepdims=True)
    store = pltpu.make_async_copy(acc, kept_hbm, loc.at[0])
    store.start()

    sums[row] = partial

    def cs_copy(target, slot):
        return pltpu.make_async_remote_copy(
            src_ref=sums.at[slot], dst_ref=sums.at[slot],
            send_sem=cs_send.at[target], recv_sem=cs_recv.at[slot],
            device_id=(target, col), device_id_type=MESH,
        )

    for d in range(1, n_row):
        cs_copy((row + d) % n_row, row).start()
    for d in range(1, n_row):
        source = (row + d) % n_row
        cs_copy(source, source).wait_recv()
    scale_ref[...] = total_rows / jnp.sum(sums[...], axis=0)

    for d in range(1, n_row):
        cs_copy((row + d) % n_row, row).wait_send()
    for p in range(2):

        @pl.when(positions[p] < n_col - 1)
        def _(p=p):
            for i in range(steps):
                a_copy(p, i // PARTS, i % PARTS, False).wait_send()

    @pl.when(positions[0] < n_col - 1)
    def _():
        ma_copy().wait_send()

    @pl.when(in_chain)
    def _():
        for i in range(steps):
            sib_copy(i // PARTS, i % PARTS).wait_send()

        @pl.when(pair > 0)
        def _():
            for i in range(steps):
                b_copy(i // PARTS, i % PARTS).wait_send()
            for s in range(SECTIONS):
                mb_copy(s, below * 2 + core, s).wait_send()

    for s in range(SECTIONS):

        @pl.when(row == n_row - SECTIONS + s)
        def _(s=s):
            for k in range(2):
                mb_copy(s, below * 2 + k, k).wait_send()
            mb_copy(s, sibling, 2).wait_send()
            for c in range(PARTS):
                for k in range(2):
                    b_root_copy(s, k, c).wait_send()
            b_root_sibling(s).wait_send()

    store.wait()


def local(n_row, n_col, a_tiles, a_index, a_count, b_tiles, b_index, b_count, c_partial, prune_mask):
    hbm = pl.BlockSpec(memory_space=pltpu.HBM)
    steps = SECTIONS * PARTS
    dma = pltpu.SemaphoreType.DMA
    rows, columns = c_partial.shape
    kept, scale = pl.pallas_call(
        functools.partial(kernel, n_row, n_col),
        out_shape=(
            jax.ShapeDtypeStruct((rows, columns), jnp.float32),
            jax.ShapeDtypeStruct((1, columns), jnp.float32),
        ),
        in_specs=[hbm] * 8,
        out_specs=(pl.BlockSpec(memory_space=pl.ANY), pl.BlockSpec(memory_space=pltpu.VMEM)),
        scratch_shapes=[
            pltpu.SMEM(a_index.shape, jnp.int32),
            pltpu.SMEM(a_count.shape, jnp.int32),
            pltpu.SMEM(b_index.shape, jnp.int32),
            pltpu.SMEM(b_count.shape, jnp.int32),
            pltpu.SMEM(prune_mask.shape, jnp.int32),
            pltpu.VMEM((KA + 1, TILE, TILE), jnp.bfloat16),
            pltpu.VMEM((KA + 1, TILE, TILE), jnp.bfloat16),
            pltpu.VMEM((KB + 1, TILE, TILE), jnp.bfloat16),
            pltpu.VMEM((KB + 1, TILE, TILE), jnp.bfloat16),
            pltpu.VMEM((2 * SECTIONS, TILE), jnp.int32),
            pltpu.VMEM((SECTIONS, KB, TILE), jnp.int32),
            pltpu.VMEM((2, TILE), jnp.int32),
            pltpu.SMEM((SECTIONS, 2, TILE), jnp.int32),
            pltpu.VMEM((rows, columns), jnp.float32),
            pltpu.VMEM((n_row, 1, columns), jnp.float32),
            dma((2, steps)), dma((2, steps)),
            dma((steps,)), dma((steps,)), dma((steps,)), dma((steps,)),
            dma((1,)), dma((1,)), dma((3,)), dma((SECTIONS,)),
            dma((n_row,)), dma((n_row,)), dma((10,)),
        ],
        compiler_params=pltpu.CompilerParams(
            collective_id=0, has_side_effects=True, vmem_limit_bytes=62 * 1024 * 1024
        ),
        cost_estimate=pl.CostEstimate(
            flops=SECTIONS * 2 * rows * KA * TILE * columns, bytes_accessed=8 * rows * columns, transcendentals=0
        ),
    )(a_index, a_count, b_index, b_count, prune_mask, a_tiles, b_tiles, c_partial)
    return kept * scale


def solution(mesh):
    n_row, n_col = mesh.shape["row"], mesh.shape["col"]
    return jax.shard_map(
        functools.partial(local, n_row, n_col),
        mesh=mesh,
        in_specs=(
            P("row", "col", None, None, None, None),
            P("row", "col", None, None),
            P("row", "col", None),
            P("row", "col", None, None, None),
            P("row", "col", None),
            P("row", "col"),
            P("row", "col"),
            P("row", "col"),
        ),
        out_specs=P("row", "col"),
        check_vma=False,
    )
```

```python
import functools

import jax
import jax.numpy as jnp
from jax import lax
from jax.experimental import pallas as pl
from jax.experimental.pallas import tpu as pltpu
from jax.sharding import PartitionSpec as P

MB = 4
NB = 4
W = 32
KA = 16
KB = 16
SECTIONS = 2
TILE = 128
STEP = 2
PARTS = KA // 2 // STEP
WINDOW = 2
LAG = 2
MESH = pl.DeviceIdType.MESH


def grid_of(n_col):
    nx = max(d for d in range(1, n_col + 1) if n_col % d == 0 and d * d <= n_col)
    return n_col // nx, nx


def snake(index, outer, inner):
    o, i = index // inner, index % inner
    return o, (1 - o % 2) * i + (o % 2) * (inner - 1 - i)


def path_position(col, path, ny, nx):
    y, x = ny - 1 - col // nx, nx - 1 - col % nx
    if path == 0:
        return y * nx + (1 - y % 2) * x + (y % 2) * (nx - 1 - x)
    return x * ny + (1 - x % 2) * y + (x % 2) * (ny - 1 - y)


def path_column(position, path, ny, nx):
    if path == 0:
        y, x = snake(position, ny, nx)
    else:
        x, y = snake(position, nx, ny)
    return (ny - 1 - y) * nx + (nx - 1 - x)


def kernel(
    n_row, n_col, ai_hbm, ac_hbm, bi_hbm, bc_hbm, mask_hbm, a_hbm, b_hbm, c_hbm,
    kept_hbm, scale_ref,
    ai_ref, ac_ref, bi_ref, bc_ref, mask_ref, lt0, lt1, rt0, rt1, ma, mb, table, table_smem, acc, sums,
    a_send, a_recv, b_send, b_recv, sib_send, sib_recv, ma_send, ma_recv, mb_send, mb_recv,
    cs_send, cs_recv, loc,
):
    row = lax.axis_index("row")
    col = lax.axis_index("col")
    pair, core = row // 2, row % 2
    last_pair = n_row // 2 - 1
    ny, nx = grid_of(n_col)
    lts, rts = (lt0, lt1), (rt0, rt1)
    total_rows = n_row * MB * TILE

    load_c = pltpu.make_async_copy(c_hbm, acc, loc.at[0])
    load_c.start()
    small = [
        pltpu.make_async_copy(source, target, loc.at[5 + i])
        for i, (source, target) in enumerate(
            ((ai_hbm, ai_ref), (ac_hbm, ac_ref), (bi_hbm, bi_ref), (bc_hbm, bc_ref), (mask_hbm, mask_ref))
        )
    ]
    for copy in small:
        copy.start()

    barrier = pltpu.get_barrier_semaphore()
    for d in range(1, n_row):
        pl.semaphore_signal(barrier, inc=1, device_id=((row + d) % n_row, col), device_id_type=MESH)
    for d in range(1, n_col):
        pl.semaphore_signal(barrier, inc=1, device_id=(row, (col + d) % n_col), device_id_type=MESH)

    for s in range(SECTIONS):
        lts[s][KA] = jnp.zeros((TILE, TILE), jnp.bfloat16)
        rts[s][KB] = jnp.zeros((TILE, TILE), jnp.bfloat16)

    for copy in small:
        copy.wait()
    lane = lax.broadcasted_iota(jnp.int32, (1, TILE), 1)

    @pl.when(col == n_col - 1)
    def _():
        for s in range(SECTIONS):
            count = ac_ref[0, 0, s]
            target = jnp.full((1, TILE), -2, jnp.int32)
            place = jnp.full((1, TILE), KA, jnp.int32)
            for a in range(KA):
                slot = ai_ref[0, 0, s, a]
                live = a < count
                inner = jnp.where(live, (slot % W) * NB, -64)
                block = jnp.where(live, slot // W, -1)
                target = jnp.where(lane // NB == a, inner + lane % NB, target)
                place = jnp.where(lane == block * KA + a, jnp.where(live, a, KA), place)
            ma[s : s + 1, :] = target
            ma[SECTIONS + s : SECTIONS + s + 1, :] = place

    for s in range(SECTIONS):

        @pl.when(row == n_row - SECTIONS + s)
        def _(s=s):
            count = bc_ref[0, 0]
            for b in range(KB):
                slot = jnp.where(b < count, bi_ref[0, 0, b], -1)
                mb[s, b : b + 1, :] = jnp.full((1, TILE), slot, jnp.int32)

    pl.semaphore_wait(barrier, n_row - 1 + n_col - 1)

    positions = [path_position(col, p, ny, nx) for p in range(2)]
    is_left_root = col == n_col - 1

    def next_col(p):
        return path_column((positions[p] + 1) % n_col, p, ny, nx)

    def a_copy(p, s, c, from_hbm):
        i = s * PARTS + c
        tiles = pl.ds(p * (KA // 2) + c * STEP, STEP)
        return pltpu.make_async_remote_copy(
            src_ref=a_hbm.at[0, 0, s, tiles] if from_hbm else lts[s].at[tiles],
            dst_ref=lts[s].at[tiles],
            send_sem=a_send.at[p, i], recv_sem=a_recv.at[p, i],
            device_id=(row, next_col(p)), device_id_type=MESH,
        )

    def ma_copy():
        return pltpu.make_async_remote_copy(
            src_ref=ma, dst_ref=ma, send_sem=ma_send.at[0], recv_sem=ma_recv.at[0],
            device_id=(row, next_col(0)), device_id_type=MESH,
        )

    def a_local(s):
        return pltpu.make_async_copy(a_hbm.at[0, 0, s], lts[s].at[pl.ds(0, KA)], loc.at[1 + s])

    below = (pair - 1 + last_pair + 1) % (last_pair + 1)
    sibling = pair * 2 + 1 - core

    def b_root_copy(s, k, c):
        tiles = pl.ds(k * (KB // 2) + c * STEP, STEP)
        return pltpu.make_async_remote_copy(
            src_ref=b_hbm.at[0, 0, tiles], dst_ref=rts[s].at[tiles],
            send_sem=b_send.at[k * PARTS + c], recv_sem=b_recv.at[s * PARTS + c],
            device_id=(below * 2 + k, col), device_id_type=MESH,
        )

    def b_root_sibling(s):
        return pltpu.make_async_remote_copy(
            src_ref=b_hbm.at[0, 0], dst_ref=rts[s].at[pl.ds(0, KB)],
            send_sem=sib_send.at[0], recv_sem=sib_recv.at[s * PARTS],
            device_id=(sibling, col), device_id_type=MESH,
        )

    def mb_copy(s, target, sem):
        return pltpu.make_async_remote_copy(
            src_ref=mb.at[s], dst_ref=mb.at[s], send_sem=mb_send.at[sem], recv_sem=mb_recv.at[s],
            device_id=(target, col), device_id_type=MESH,
        )

    def b_chain_copy(s, c, k, target, send, recv):
        ref = rts[s].at[pl.ds(k * (KB // 2) + c * STEP, STEP)]
        i = s * PARTS + c
        return pltpu.make_async_remote_copy(
            src_ref=ref, dst_ref=ref, send_sem=send.at[i], recv_sem=recv.at[i],
            device_id=(target, col), device_id_type=MESH,
        )

    def b_copy(s, c):
        return b_chain_copy(s, c, core, below * 2 + core, b_send, b_recv)

    def sib_copy(s, c):
        return b_chain_copy(s, c, core, sibling, sib_send, sib_recv)

    def sib_arrival(s, c):
        return b_chain_copy(s, c, 1 - core, sibling, sib_send, sib_recv)

    def b_local(s):
        return pltpu.make_async_copy(b_hbm.at[0, 0], rts[s].at[pl.ds(0, KB)], loc.at[3])

    steps = SECTIONS * PARTS
    in_chain = pair < last_pair

    @pl.when(is_left_root)
    def _():
        ma_copy().start()

    for s in range(SECTIONS):

        @pl.when(row == n_row - SECTIONS + s)
        def _(s=s):
            for k in range(2):
                mb_copy(s, below * 2 + k, k).start()
            mb_copy(s, sibling, 2).start()

    def forward(t):
        if t < steps:

            @pl.when(is_left_root)
            def _():
                for p in range(2):
                    if t >= WINDOW:
                        a_copy(p, (t - WINDOW) // PARTS, (t - WINDOW) % PARTS, True).wait_send()
                    a_copy(p, t // PARTS, t % PARTS, True).start()

            @pl.when(row == n_row - SECTIONS + t // PARTS)
            def _():
                s, c = t // PARTS, t % PARTS
                for k in range(2):
                    if c >= WINDOW:
                        b_root_copy(s, k, c - WINDOW).wait_send()
                    b_root_copy(s, k, c).start()

        if t == 0:

            @pl.when(is_left_root)
            def _():
                for s in range(SECTIONS):
                    a_local(s).start()

            for s in range(SECTIONS):

                @pl.when(row == n_row - SECTIONS + s)
                def _(s=s):
                    b_root_sibling(s).start()
                    b_local(s).start()

        for p in range(2):
            i = t - LAG * (positions[p] - 1)
            passes = (positions[p] > 0) & (positions[p] < n_col - 1)
            if p == 0:

                @pl.when(passes & (i == 0))
                def _():
                    ma_copy().wait_recv()
                    ma_copy().start()

            for s in range(SECTIONS):
                c = i - s * PARTS

                @pl.when(passes & (c >= 0) & (c < PARTS))
                def _(p=p, s=s, c=c):
                    a_copy(p, s, c, False).wait_recv()
                    a_copy(p, s, c, False).start()

        i = t - LAG * (last_pair - 1 - pair)
        for s in range(SECTIONS):
            c = i - s * PARTS

            @pl.when(in_chain & (c == 0))
            def _(s=s):
                mb_copy(s, below * 2 + core, s).wait_recv()

                @pl.when(pair > 0)
                def _():
                    mb_copy(s, below * 2 + core, s).start()

            @pl.when(in_chain & (c >= 0) & (c < PARTS))
            def _(s=s, c=c):
                b_copy(s, c).wait_recv()

                @pl.when(pair > 0)
                def _():
                    b_copy(s, c).start()

                sib_copy(s, c).start()

    def section_ready(s):
        for p in range(2):

            @pl.when(positions[p] == n_col - 1)
            def _(p=p):
                for c in range(PARTS):
                    a_copy(p, s, c, False).wait_recv()

        @pl.when(is_left_root)
        def _():
            a_local(s).wait()

        @pl.when(in_chain)
        def _():
            for c in range(PARTS):
                sib_arrival(s, c).wait_recv()

        @pl.when(row == n_row - SECTIONS + s)
        def _():
            b_local(s).wait()

        @pl.when(row == n_row - 1 - s)
        def _():
            b_root_sibling(s).wait_recv()

    most = LAG * max(n_col - 3, last_pair - 1, 0)
    for t in range(PARTS + most):
        forward(t)

    @pl.when(positions[0] == n_col - 1)
    def _():
        ma_copy().wait_recv()

    for s in range(SECTIONS):
        @pl.when(row == n_row - 1 - s)
        def _(s=s):
            mb_copy(s, sibling, s).wait_recv()

    group = KA // PARTS

    def product(s, j):
        left = jnp.concatenate(
            [
                jnp.concatenate(
                    [lts[s][table_smem[s, 1, m * KA + j * group + a]] for a in range(group)],
                    axis=1,
                )
                for m in range(MB)
            ],
            axis=0,
        )
        right = jnp.concatenate(
            [
                jnp.concatenate(
                    [rts[s][table_smem[s, 0, (j * group + a) * NB + n]] for n in range(NB)], axis=1
                )
                for a in range(group)
            ],
            axis=0,
        )
        acc[...] += jnp.dot(left, right, preferred_element_type=jnp.float32)

    row_id = lax.broadcasted_iota(jnp.int32, (KB, TILE), 0)

    def make_table(s):
        table[0:1, :] = jnp.min(jnp.where(mb[s] == ma[s : s + 1, :], row_id, KB), axis=0, keepdims=True)
        table[1:2, :] = ma[SECTIONS + s : SECTIONS + s + 1, :]
        to_smem = pltpu.make_async_copy(table, table_smem.at[s], loc.at[4])
        to_smem.start()
        to_smem.wait()

    load_c.wait()
    for s in range(SECTIONS):
        section_ready(s)
        make_table(s)
        for j in range(PARTS):
            if s + 1 < SECTIONS:
                forward(PARTS + most + j)
            product(s, j)

    partial = jnp.zeros((1, NB * TILE), jnp.float32)
    for m in range(MB):
        keep = jnp.concatenate(
            [
                jnp.full((1, TILE), mask_ref[m, n].astype(jnp.float32), jnp.float32)
                for n in range(NB)
            ],
            axis=1,
        )
        block = acc[m * TILE : (m + 1) * TILE, :]
        kept = block * block * keep
        acc[m * TILE : (m + 1) * TILE, :] = kept
        partial = partial + jnp.sum(kept, axis=0, keepdims=True)
    store = pltpu.make_async_copy(acc, kept_hbm, loc.at[0])
    store.start()

    sums[row] = partial

    def cs_copy(target, slot):
        return pltpu.make_async_remote_copy(
            src_ref=sums.at[slot], dst_ref=sums.at[slot],
            send_sem=cs_send.at[target], recv_sem=cs_recv.at[slot],
            device_id=(target, col), device_id_type=MESH,
        )

    for d in range(1, n_row):
        cs_copy((row + d) % n_row, row).start()
    for d in range(1, n_row):
        source = (row + d) % n_row
        cs_copy(source, source).wait_recv()
    scale_ref[...] = total_rows / jnp.sum(sums[...], axis=0)

    for d in range(1, n_row):
        cs_copy((row + d) % n_row, row).wait_send()
    for p in range(2):

        @pl.when((positions[p] > 0) & (positions[p] < n_col - 1))
        def _(p=p):
            for i in range(steps):
                a_copy(p, i // PARTS, i % PARTS, False).wait_send()

        @pl.when(is_left_root)
        def _(p=p):
            for i in range(steps - WINDOW, steps):
                a_copy(p, i // PARTS, i % PARTS, True).wait_send()

    @pl.when(positions[0] < n_col - 1)
    def _():
        ma_copy().wait_send()

    @pl.when(in_chain)
    def _():
        for i in range(steps):
            sib_copy(i // PARTS, i % PARTS).wait_send()

        @pl.when(pair > 0)
        def _():
            for i in range(steps):
                b_copy(i // PARTS, i % PARTS).wait_send()
            for s in range(SECTIONS):
                mb_copy(s, below * 2 + core, s).wait_send()

    for s in range(SECTIONS):

        @pl.when(row == n_row - SECTIONS + s)
        def _(s=s):
            for k in range(2):
                mb_copy(s, below * 2 + k, k).wait_send()
            mb_copy(s, sibling, 2).wait_send()
            for c in range(PARTS - WINDOW, PARTS):
                for k in range(2):
                    b_root_copy(s, k, c).wait_send()
            b_root_sibling(s).wait_send()

    store.wait()


def local(n_row, n_col, a_tiles, a_index, a_count, b_tiles, b_index, b_count, c_partial, prune_mask):
    hbm = pl.BlockSpec(memory_space=pltpu.HBM)
    steps = SECTIONS * PARTS
    dma = pltpu.SemaphoreType.DMA
    rows, columns = c_partial.shape
    kept, scale = pl.pallas_call(
        functools.partial(kernel, n_row, n_col),
        out_shape=(
            jax.ShapeDtypeStruct((rows, columns), jnp.float32),
            jax.ShapeDtypeStruct((1, columns), jnp.float32),
        ),
        in_specs=[hbm] * 8,
        out_specs=(pl.BlockSpec(memory_space=pl.ANY), pl.BlockSpec(memory_space=pltpu.VMEM)),
        scratch_shapes=[
            pltpu.SMEM(a_index.shape, jnp.int32),
            pltpu.SMEM(a_count.shape, jnp.int32),
            pltpu.SMEM(b_index.shape, jnp.int32),
            pltpu.SMEM(b_count.shape, jnp.int32),
            pltpu.SMEM(prune_mask.shape, jnp.int32),
            pltpu.VMEM((KA + 1, TILE, TILE), jnp.bfloat16),
            pltpu.VMEM((KA + 1, TILE, TILE), jnp.bfloat16),
            pltpu.VMEM((KB + 1, TILE, TILE), jnp.bfloat16),
            pltpu.VMEM((KB + 1, TILE, TILE), jnp.bfloat16),
            pltpu.VMEM((2 * SECTIONS, TILE), jnp.int32),
            pltpu.VMEM((SECTIONS, KB, TILE), jnp.int32),
            pltpu.VMEM((2, TILE), jnp.int32),
            pltpu.SMEM((SECTIONS, 2, TILE), jnp.int32),
            pltpu.VMEM((rows, columns), jnp.float32),
            pltpu.VMEM((n_row, 1, columns), jnp.float32),
            dma((2, steps)), dma((2, steps)),
            dma((steps,)), dma((steps,)), dma((steps,)), dma((steps,)),
            dma((1,)), dma((1,)), dma((3,)), dma((SECTIONS,)),
            dma((n_row,)), dma((n_row,)), dma((10,)),
        ],
        compiler_params=pltpu.CompilerParams(
            collective_id=0, has_side_effects=True, vmem_limit_bytes=62 * 1024 * 1024
        ),
        cost_estimate=pl.CostEstimate(
            flops=SECTIONS * 2 * rows * KA * TILE * columns, bytes_accessed=8 * rows * columns, transcendentals=0
        ),
    )(a_index, a_count, b_index, b_count, prune_mask, a_tiles, b_tiles, c_partial)
    return kept * scale


def solution(mesh):
    n_row, n_col = mesh.shape["row"], mesh.shape["col"]
    return jax.shard_map(
        functools.partial(local, n_row, n_col),
        mesh=mesh,
        in_specs=(
            P("row", "col", None, None, None, None),
            P("row", "col", None, None),
            P("row", "col", None),
            P("row", "col", None, None, None),
            P("row", "col", None),
            P("row", "col"),
            P("row", "col"),
            P("row", "col"),
        ),
        out_specs=P("row", "col"),
        check_vma=False,
    )
```

```python
import functools

import jax
import jax.numpy as jnp
from jax import lax
from jax.experimental import pallas as pl
from jax.experimental.pallas import tpu as pltpu
from jax.sharding import PartitionSpec as P

MB = 4
NB = 4
W = 32
KA = 16
KB = 16
SECTIONS = 2
TILE = 128
STEP = 2
PARTS = KA // 2 // STEP
WINDOW = 2
LAG = 2
MESH = pl.DeviceIdType.MESH


def grid_of(n_col):
    nx = max(d for d in range(1, n_col + 1) if n_col % d == 0 and d * d <= n_col)
    return n_col // nx, nx


def snake(index, outer, inner):
    o, i = index // inner, index % inner
    return o, (1 - o % 2) * i + (o % 2) * (inner - 1 - i)


def path_position(col, path, ny, nx):
    y, x = ny - 1 - col // nx, nx - 1 - col % nx
    if path == 0:
        return y * nx + (1 - y % 2) * x + (y % 2) * (nx - 1 - x)
    return x * ny + (1 - x % 2) * y + (x % 2) * (ny - 1 - y)


def path_column(position, path, ny, nx):
    if path == 0:
        y, x = snake(position, ny, nx)
    else:
        x, y = snake(position, nx, ny)
    return (ny - 1 - y) * nx + (nx - 1 - x)


def kernel(
    n_row, n_col, ai_hbm, ac_hbm, bi_hbm, bc_hbm, mask_hbm, a_hbm, b_hbm, c_hbm,
    acc, scale_ref,
    ai_ref, ac_ref, bi_ref, bc_ref, mask_ref, lt0, lt1, rt0, rt1, ma, mb, table, table_smem, sums,
    a_send, a_recv, b_send, b_recv, sib_send, sib_recv, ma_send, ma_recv, mb_send, mb_recv,
    cs_send, cs_recv, loc,
):
    row = lax.axis_index("row")
    col = lax.axis_index("col")
    pair, core = row // 2, row % 2
    last_pair = n_row // 2 - 1
    ny, nx = grid_of(n_col)
    lts, rts = (lt0, lt1), (rt0, rt1)
    total_rows = n_row * MB * TILE

    load_c = pltpu.make_async_copy(c_hbm, acc, loc.at[0])
    load_c.start()
    small = [
        pltpu.make_async_copy(source, target, loc.at[5 + i])
        for i, (source, target) in enumerate(
            ((ai_hbm, ai_ref), (ac_hbm, ac_ref), (bi_hbm, bi_ref), (bc_hbm, bc_ref), (mask_hbm, mask_ref))
        )
    ]
    for copy in small:
        copy.start()

    barrier = pltpu.get_barrier_semaphore()
    for d in range(1, n_row):
        pl.semaphore_signal(barrier, inc=1, device_id=((row + d) % n_row, col), device_id_type=MESH)
    for d in range(1, n_col):
        pl.semaphore_signal(barrier, inc=1, device_id=(row, (col + d) % n_col), device_id_type=MESH)

    for s in range(SECTIONS):
        lts[s][KA] = jnp.zeros((TILE, TILE), jnp.bfloat16)
        rts[s][KB] = jnp.zeros((TILE, TILE), jnp.bfloat16)

    pl.semaphore_wait(barrier, n_row - 1 + n_col - 1)

    positions = [path_position(col, p, ny, nx) for p in range(2)]
    is_left_root = col == n_col - 1

    def next_col(p):
        return path_column((positions[p] + 1) % n_col, p, ny, nx)

    def a_copy(p, s, c, from_hbm):
        i = s * PARTS + c
        tiles = pl.ds(p * (KA // 2) + c * STEP, STEP)
        return pltpu.make_async_remote_copy(
            src_ref=a_hbm.at[0, 0, s, tiles] if from_hbm else lts[s].at[tiles],
            dst_ref=lts[s].at[tiles],
            send_sem=a_send.at[p, i], recv_sem=a_recv.at[p, i],
            device_id=(row, next_col(p)), device_id_type=MESH,
        )

    def ma_copy():
        return pltpu.make_async_remote_copy(
            src_ref=ma, dst_ref=ma, send_sem=ma_send.at[0], recv_sem=ma_recv.at[0],
            device_id=(row, next_col(0)), device_id_type=MESH,
        )

    def a_local(s):
        return pltpu.make_async_copy(a_hbm.at[0, 0, s], lts[s].at[pl.ds(0, KA)], loc.at[1 + s])

    below = (pair - 1 + last_pair + 1) % (last_pair + 1)
    sibling = pair * 2 + 1 - core

    def b_root_copy(s, k, c):
        tiles = pl.ds(k * (KB // 2) + c * STEP, STEP)
        return pltpu.make_async_remote_copy(
            src_ref=b_hbm.at[0, 0, tiles], dst_ref=rts[s].at[tiles],
            send_sem=b_send.at[k * PARTS + c], recv_sem=b_recv.at[s * PARTS + c],
            device_id=(below * 2 + k, col), device_id_type=MESH,
        )

    def b_root_sibling(s):
        return pltpu.make_async_remote_copy(
            src_ref=b_hbm.at[0, 0], dst_ref=rts[s].at[pl.ds(0, KB)],
            send_sem=sib_send.at[0], recv_sem=sib_recv.at[s * PARTS],
            device_id=(sibling, col), device_id_type=MESH,
        )

    def mb_copy(s, target, sem):
        return pltpu.make_async_remote_copy(
            src_ref=mb.at[s], dst_ref=mb.at[s], send_sem=mb_send.at[sem], recv_sem=mb_recv.at[s],
            device_id=(target, col), device_id_type=MESH,
        )

    def b_chain_copy(s, c, k, target, send, recv):
        ref = rts[s].at[pl.ds(k * (KB // 2) + c * STEP, STEP)]
        i = s * PARTS + c
        return pltpu.make_async_remote_copy(
            src_ref=ref, dst_ref=ref, send_sem=send.at[i], recv_sem=recv.at[i],
            device_id=(target, col), device_id_type=MESH,
        )

    def b_copy(s, c):
        return b_chain_copy(s, c, core, below * 2 + core, b_send, b_recv)

    def sib_copy(s, c):
        return b_chain_copy(s, c, core, sibling, sib_send, sib_recv)

    def sib_arrival(s, c):
        return b_chain_copy(s, c, 1 - core, sibling, sib_send, sib_recv)

    def b_local(s):
        return pltpu.make_async_copy(b_hbm.at[0, 0], rts[s].at[pl.ds(0, KB)], loc.at[3])

    steps = SECTIONS * PARTS
    in_chain = pair < last_pair

    def root_start(t):
        if t < steps:

            @pl.when(is_left_root)
            def _():
                for p in range(2):
                    if t >= WINDOW:
                        a_copy(p, (t - WINDOW) // PARTS, (t - WINDOW) % PARTS, True).wait_send()
                    a_copy(p, t // PARTS, t % PARTS, True).start()

        for s in range(SECTIONS):
            c = t - WINDOW * s
            if 0 <= c < PARTS:

                @pl.when(row == n_row - SECTIONS + s)
                def _(s=s, c=c):
                    for k in range(2):
                        if c >= WINDOW:
                            b_root_copy(s, k, c - WINDOW).wait_send()
                        b_root_copy(s, k, c).start()

    for t in range(WINDOW):
        root_start(t)

    @pl.when(is_left_root)
    def _():
        for s in range(SECTIONS):
            a_local(s).start()

    for s in range(SECTIONS):

        @pl.when(row == n_row - SECTIONS + s)
        def _(s=s):
            b_root_sibling(s).start()
            b_local(s).start()

    for copy in small:
        copy.wait()
    lane = lax.broadcasted_iota(jnp.int32, (1, TILE), 1)

    @pl.when(col == n_col - 1)
    def _():
        for s in range(SECTIONS):
            count = ac_ref[0, 0, s]
            target = jnp.full((1, TILE), -2, jnp.int32)
            place = jnp.full((1, TILE), KA, jnp.int32)
            for a in range(KA):
                slot = ai_ref[0, 0, s, a]
                live = a < count
                inner = jnp.where(live, (slot % W) * NB, -64)
                block = jnp.where(live, slot // W, -1)
                target = jnp.where(lane // NB == a, inner + lane % NB, target)
                place = jnp.where(lane == block * KA + a, jnp.where(live, a, KA), place)
            ma[s : s + 1, :] = target
            ma[SECTIONS + s : SECTIONS + s + 1, :] = place

    for s in range(SECTIONS):

        @pl.when(row == n_row - SECTIONS + s)
        def _(s=s):
            count = bc_ref[0, 0]
            for b in range(KB):
                slot = jnp.where(b < count, bi_ref[0, 0, b], -1)
                mb[s, b : b + 1, :] = jnp.full((1, TILE), slot, jnp.int32)

    @pl.when(is_left_root)
    def _():
        ma_copy().start()

    for s in range(SECTIONS):

        @pl.when(row == n_row - SECTIONS + s)
        def _(s=s):
            for k in range(2):
                mb_copy(s, below * 2 + k, k).start()
            mb_copy(s, sibling, 2).start()

    def forward(t):
        root_start(t + WINDOW)
        for p in range(2):
            i = t - LAG * (positions[p] - 1)
            passes = (positions[p] > 0) & (positions[p] < n_col - 1)
            for s in range(SECTIONS):
                c = i - s * PARTS

                @pl.when(passes & (c >= 0) & (c < PARTS))
                def _(p=p, s=s, c=c):
                    a_copy(p, s, c, False).wait_recv()
                    a_copy(p, s, c, False).start()

            if p == 0:

                @pl.when(passes & (i == 1))
                def _():
                    ma_copy().wait_recv()
                    ma_copy().start()

        i = t - LAG * (last_pair - 1 - pair)
        for s in range(SECTIONS):
            c = i - s * PARTS

            @pl.when(in_chain & (c >= 0) & (c < PARTS))
            def _(s=s, c=c):
                b_copy(s, c).wait_recv()

                @pl.when(pair > 0)
                def _():
                    b_copy(s, c).start()

                sib_copy(s, c).start()

            @pl.when(in_chain & (c == 1))
            def _(s=s):
                mb_copy(s, below * 2 + core, s).wait_recv()

                @pl.when(pair > 0)
                def _():
                    mb_copy(s, below * 2 + core, s).start()

    def section_ready(s):
        for p in range(2):

            @pl.when(positions[p] == n_col - 1)
            def _(p=p):
                for c in range(PARTS):
                    a_copy(p, s, c, False).wait_recv()

        @pl.when(is_left_root)
        def _():
            a_local(s).wait()

        @pl.when(in_chain)
        def _():
            for c in range(PARTS):
                sib_arrival(s, c).wait_recv()

        @pl.when(row == n_row - SECTIONS + s)
        def _():
            b_local(s).wait()

        @pl.when(row == n_row - 1 - s)
        def _():
            b_root_sibling(s).wait_recv()

    most = LAG * max(n_col - 3, last_pair - 1, 0)
    for t in range(PARTS + most):
        forward(t)

    @pl.when(positions[0] == n_col - 1)
    def _():
        ma_copy().wait_recv()

    for s in range(SECTIONS):
        @pl.when(row == n_row - 1 - s)
        def _(s=s):
            mb_copy(s, sibling, s).wait_recv()

    group = KA // PARTS

    def product(s, j):
        left = jnp.concatenate(
            [
                jnp.concatenate(
                    [lts[s][table_smem[s, 1, m * KA + j * group + a]] for a in range(group)],
                    axis=1,
                )
                for m in range(MB)
            ],
            axis=0,
        )
        right = jnp.concatenate(
            [
                jnp.concatenate(
                    [rts[s][table_smem[s, 0, (j * group + a) * NB + n]] for n in range(NB)], axis=1
                )
                for a in range(group)
            ],
            axis=0,
        )
        acc[...] += jnp.dot(left, right, preferred_element_type=jnp.float32)

    row_id = lax.broadcasted_iota(jnp.int32, (KB, TILE), 0)

    def make_table(s):
        table[0:1, :] = jnp.min(jnp.where(mb[s] == ma[s : s + 1, :], row_id, KB), axis=0, keepdims=True)
        table[1:2, :] = ma[SECTIONS + s : SECTIONS + s + 1, :]
        to_smem = pltpu.make_async_copy(table, table_smem.at[s], loc.at[4])
        to_smem.start()
        to_smem.wait()

    load_c.wait()
    for s in range(SECTIONS):
        section_ready(s)
        make_table(s)
        for j in range(PARTS):
            if s + 1 < SECTIONS:
                forward(PARTS + most + j)
            product(s, j)

    partial = jnp.zeros((1, NB * TILE), jnp.float32)
    for m in range(MB):
        keep = jnp.concatenate(
            [
                jnp.full((1, TILE), mask_ref[m, n].astype(jnp.float32), jnp.float32)
                for n in range(NB)
            ],
            axis=1,
        )
        block = acc[m * TILE : (m + 1) * TILE, :]
        kept = block * block * keep
        acc[m * TILE : (m + 1) * TILE, :] = kept
        partial = partial + jnp.sum(kept, axis=0, keepdims=True)
    sums[row] = partial

    def cs_copy(target, slot):
        return pltpu.make_async_remote_copy(
            src_ref=sums.at[slot], dst_ref=sums.at[slot],
            send_sem=cs_send.at[target], recv_sem=cs_recv.at[slot],
            device_id=(target, col), device_id_type=MESH,
        )

    for d in range(1, n_row):
        cs_copy((row + d) % n_row, row).start()
    for d in range(1, n_row):
        source = (row + d) % n_row
        cs_copy(source, source).wait_recv()
    scale_ref[...] = total_rows / jnp.sum(sums[...], axis=0)

    for d in range(1, n_row):
        cs_copy((row + d) % n_row, row).wait_send()
    for p in range(2):

        @pl.when((positions[p] > 0) & (positions[p] < n_col - 1))
        def _(p=p):
            for i in range(steps):
                a_copy(p, i // PARTS, i % PARTS, False).wait_send()

        @pl.when(is_left_root)
        def _(p=p):
            for i in range(steps - WINDOW, steps):
                a_copy(p, i // PARTS, i % PARTS, True).wait_send()

    @pl.when(positions[0] < n_col - 1)
    def _():
        ma_copy().wait_send()

    @pl.when(in_chain)
    def _():
        for i in range(steps):
            sib_copy(i // PARTS, i % PARTS).wait_send()

        @pl.when(pair > 0)
        def _():
            for i in range(steps):
                b_copy(i // PARTS, i % PARTS).wait_send()
            for s in range(SECTIONS):
                mb_copy(s, below * 2 + core, s).wait_send()

    for s in range(SECTIONS):

        @pl.when(row == n_row - SECTIONS + s)
        def _(s=s):
            for k in range(2):
                mb_copy(s, below * 2 + k, k).wait_send()
            mb_copy(s, sibling, 2).wait_send()
            for c in range(PARTS - WINDOW, PARTS):
                for k in range(2):
                    b_root_copy(s, k, c).wait_send()
            b_root_sibling(s).wait_send()


def local(n_row, n_col, a_tiles, a_index, a_count, b_tiles, b_index, b_count, c_partial, prune_mask):
    hbm = pl.BlockSpec(memory_space=pltpu.HBM)
    steps = SECTIONS * PARTS
    dma = pltpu.SemaphoreType.DMA
    rows, columns = c_partial.shape
    kept, scale = pl.pallas_call(
        functools.partial(kernel, n_row, n_col),
        out_shape=(
            pltpu.VMEM((rows, columns), jnp.float32),
            pltpu.VMEM((1, columns), jnp.float32),
        ),
        in_specs=[hbm] * 8,
        out_specs=(pl.BlockSpec(memory_space=pltpu.VMEM), pl.BlockSpec(memory_space=pltpu.VMEM)),
        scratch_shapes=[
            pltpu.SMEM(a_index.shape, jnp.int32),
            pltpu.SMEM(a_count.shape, jnp.int32),
            pltpu.SMEM(b_index.shape, jnp.int32),
            pltpu.SMEM(b_count.shape, jnp.int32),
            pltpu.SMEM(prune_mask.shape, jnp.int32),
            pltpu.VMEM((KA + 1, TILE, TILE), jnp.bfloat16),
            pltpu.VMEM((KA + 1, TILE, TILE), jnp.bfloat16),
            pltpu.VMEM((KB + 1, TILE, TILE), jnp.bfloat16),
            pltpu.VMEM((KB + 1, TILE, TILE), jnp.bfloat16),
            pltpu.VMEM((2 * SECTIONS, TILE), jnp.int32),
            pltpu.VMEM((SECTIONS, KB, TILE), jnp.int32),
            pltpu.VMEM((2, TILE), jnp.int32),
            pltpu.SMEM((SECTIONS, 2, TILE), jnp.int32),
            pltpu.VMEM((n_row, 1, columns), jnp.float32),
            dma((2, steps)), dma((2, steps)),
            dma((steps,)), dma((steps,)), dma((steps,)), dma((steps,)),
            dma((1,)), dma((1,)), dma((3,)), dma((SECTIONS,)),
            dma((n_row,)), dma((n_row,)), dma((10,)),
        ],
        compiler_params=pltpu.CompilerParams(
            collective_id=0, has_side_effects=True, vmem_limit_bytes=60 * 1024 * 1024
        ),
        cost_estimate=pl.CostEstimate(
            flops=SECTIONS * 2 * rows * KA * TILE * columns, bytes_accessed=8 * rows * columns, transcendentals=0
        ),
    )(a_index, a_count, b_index, b_count, prune_mask, a_tiles, b_tiles, c_partial)
    return kept * scale


def solution(mesh):
    n_row, n_col = mesh.shape["row"], mesh.shape["col"]
    return jax.shard_map(
        functools.partial(local, n_row, n_col),
        mesh=mesh,
        in_specs=(
            P("row", "col", None, None, None, None),
            P("row", "col", None, None),
            P("row", "col", None),
            P("row", "col", None, None, None),
            P("row", "col", None),
            P("row", "col"),
            P("row", "col"),
            P("row", "col"),
        ),
        out_specs=P("row", "col"),
        check_vma=False,
    )
```

```python
import functools

import jax
import jax.numpy as jnp
from jax import lax
from jax.experimental import pallas as pl
from jax.experimental.pallas import tpu as pltpu
from jax.sharding import PartitionSpec as P

MB = 4
NB = 4
W = 32
KA = 16
KB = 16
SECTIONS = 2
TILE = 128
STEP = 1
PARTS = KA // 2 // STEP
WINDOW = 3
LAG = 3
MESH = pl.DeviceIdType.MESH


def grid_of(n_col):
    nx = max(d for d in range(1, n_col + 1) if n_col % d == 0 and d * d <= n_col)
    return n_col // nx, nx


def snake(index, outer, inner):
    o, i = index // inner, index % inner
    return o, (1 - o % 2) * i + (o % 2) * (inner - 1 - i)


def path_position(col, path, ny, nx):
    y, x = ny - 1 - col // nx, nx - 1 - col % nx
    if path == 0:
        return y * nx + (1 - y % 2) * x + (y % 2) * (nx - 1 - x)
    return x * ny + (1 - x % 2) * y + (x % 2) * (ny - 1 - y)


def path_column(position, path, ny, nx):
    if path == 0:
        y, x = snake(position, ny, nx)
    else:
        x, y = snake(position, nx, ny)
    return (ny - 1 - y) * nx + (nx - 1 - x)


def kernel(
    n_row, n_col, ai_hbm, ac_hbm, bi_hbm, bc_hbm, mask_hbm, a_hbm, b_hbm, c_hbm,
    acc, scale_ref,
    ai_ref, ac_ref, bi_ref, bc_ref, mask_ref, lt0, lt1, rt0, rt1, ma, mb, table, table_smem, sums,
    a_send, a_recv, b_send, b_recv, sib_send, sib_recv, ma_send, ma_recv, mb_send, mb_recv,
    cs_send, cs_recv, loc,
):
    row = lax.axis_index("row")
    col = lax.axis_index("col")
    pair, core = row // 2, row % 2
    last_pair = n_row // 2 - 1
    ny, nx = grid_of(n_col)
    lts, rts = (lt0, lt1), (rt0, rt1)
    total_rows = n_row * MB * TILE

    load_c = pltpu.make_async_copy(c_hbm, acc, loc.at[0])
    load_c.start()
    small = [
        pltpu.make_async_copy(source, target, loc.at[5 + i])
        for i, (source, target) in enumerate(
            ((ai_hbm, ai_ref), (ac_hbm, ac_ref), (bi_hbm, bi_ref), (bc_hbm, bc_ref), (mask_hbm, mask_ref))
        )
    ]
    for copy in small:
        copy.start()

    barrier = pltpu.get_barrier_semaphore()
    for d in range(1, n_row):
        pl.semaphore_signal(barrier, inc=1, device_id=((row + d) % n_row, col), device_id_type=MESH)
    for d in range(1, n_col):
        pl.semaphore_signal(barrier, inc=1, device_id=(row, (col + d) % n_col), device_id_type=MESH)

    for s in range(SECTIONS):
        lts[s][KA] = jnp.zeros((TILE, TILE), jnp.bfloat16)
        rts[s][KB] = jnp.zeros((TILE, TILE), jnp.bfloat16)

    pl.semaphore_wait(barrier, n_row - 1 + n_col - 1)

    positions = [path_position(col, p, ny, nx) for p in range(2)]
    is_left_root = col == n_col - 1

    def next_col(p):
        return path_column((positions[p] + 1) % n_col, p, ny, nx)

    def a_copy(p, s, c, from_hbm):
        i = s * PARTS + c
        tiles = pl.ds(p * (KA // 2) + c * STEP, STEP)
        return pltpu.make_async_remote_copy(
            src_ref=a_hbm.at[0, 0, s, tiles] if from_hbm else lts[s].at[tiles],
            dst_ref=lts[s].at[tiles],
            send_sem=a_send.at[p, i], recv_sem=a_recv.at[p, i],
            device_id=(row, next_col(p)), device_id_type=MESH,
        )

    def ma_copy():
        return pltpu.make_async_remote_copy(
            src_ref=ma, dst_ref=ma, send_sem=ma_send.at[0], recv_sem=ma_recv.at[0],
            device_id=(row, next_col(0)), device_id_type=MESH,
        )

    def a_local(s):
        return pltpu.make_async_copy(a_hbm.at[0, 0, s], lts[s].at[pl.ds(0, KA)], loc.at[1 + s])

    below = (pair - 1 + last_pair + 1) % (last_pair + 1)
    sibling = pair * 2 + 1 - core

    def b_root_copy(s, k, c):
        tiles = pl.ds(k * (KB // 2) + c * STEP, STEP)
        return pltpu.make_async_remote_copy(
            src_ref=b_hbm.at[0, 0, tiles], dst_ref=rts[s].at[tiles],
            send_sem=b_send.at[k * PARTS + c], recv_sem=b_recv.at[s * PARTS + c],
            device_id=(below * 2 + k, col), device_id_type=MESH,
        )

    def b_root_sibling(s):
        return pltpu.make_async_remote_copy(
            src_ref=b_hbm.at[0, 0], dst_ref=rts[s].at[pl.ds(0, KB)],
            send_sem=sib_send.at[0], recv_sem=sib_recv.at[s * PARTS],
            device_id=(sibling, col), device_id_type=MESH,
        )

    def mb_copy(s, target, sem):
        return pltpu.make_async_remote_copy(
            src_ref=mb.at[s], dst_ref=mb.at[s], send_sem=mb_send.at[sem], recv_sem=mb_recv.at[s],
            device_id=(target, col), device_id_type=MESH,
        )

    def b_chain_copy(s, c, k, target, send, recv):
        ref = rts[s].at[pl.ds(k * (KB // 2) + c * STEP, STEP)]
        i = s * PARTS + c
        return pltpu.make_async_remote_copy(
            src_ref=ref, dst_ref=ref, send_sem=send.at[i], recv_sem=recv.at[i],
            device_id=(target, col), device_id_type=MESH,
        )

    def b_copy(s, c):
        return b_chain_copy(s, c, core, below * 2 + core, b_send, b_recv)

    def sib_copy(s, c):
        return b_chain_copy(s, c, core, sibling, sib_send, sib_recv)

    def sib_arrival(s, c):
        return b_chain_copy(s, c, 1 - core, sibling, sib_send, sib_recv)

    def b_local(s):
        return pltpu.make_async_copy(b_hbm.at[0, 0], rts[s].at[pl.ds(0, KB)], loc.at[3])

    steps = SECTIONS * PARTS
    in_chain = pair < last_pair

    def root_start(t):
        if t < steps:

            @pl.when(is_left_root)
            def _():
                for p in range(2):
                    if t >= WINDOW:
                        a_copy(p, (t - WINDOW) // PARTS, (t - WINDOW) % PARTS, True).wait_send()
                    a_copy(p, t // PARTS, t % PARTS, True).start()

        for s in range(SECTIONS):
            c = t - PARTS // 2 * s
            if 0 <= c < PARTS:

                @pl.when(row == n_row - SECTIONS + s)
                def _(s=s, c=c):
                    for k in range(2):
                        if c >= WINDOW:
                            b_root_copy(s, k, c - WINDOW).wait_send()
                        b_root_copy(s, k, c).start()

    for t in range(WINDOW):
        root_start(t)

    @pl.when(is_left_root)
    def _():
        for s in range(SECTIONS):
            a_local(s).start()

    for s in range(SECTIONS):

        @pl.when(row == n_row - SECTIONS + s)
        def _(s=s):
            b_root_sibling(s).start()
            b_local(s).start()

    for copy in small:
        copy.wait()
    lane = lax.broadcasted_iota(jnp.int32, (1, TILE), 1)

    @pl.when(col == n_col - 1)
    def _():
        for s in range(SECTIONS):
            count = ac_ref[0, 0, s]
            target = jnp.full((1, TILE), -2, jnp.int32)
            place = jnp.full((1, TILE), KA, jnp.int32)
            for a in range(KA):
                slot = ai_ref[0, 0, s, a]
                live = a < count
                inner = jnp.where(live, (slot % W) * NB, -64)
                block = jnp.where(live, slot // W, -1)
                target = jnp.where(lane // NB == a, inner + lane % NB, target)
                place = jnp.where(lane == block * KA + a, jnp.where(live, a, KA), place)
            ma[s : s + 1, :] = target
            ma[SECTIONS + s : SECTIONS + s + 1, :] = place

    for s in range(SECTIONS):

        @pl.when(row == n_row - SECTIONS + s)
        def _(s=s):
            count = bc_ref[0, 0]
            for b in range(KB):
                slot = jnp.where(b < count, bi_ref[0, 0, b], -1)
                mb[s, b : b + 1, :] = jnp.full((1, TILE), slot, jnp.int32)

    @pl.when(is_left_root)
    def _():
        ma_copy().start()

    for s in range(SECTIONS):

        @pl.when(row == n_row - SECTIONS + s)
        def _(s=s):
            for k in range(2):
                mb_copy(s, below * 2 + k, k).start()
            mb_copy(s, sibling, 2).start()

    def forward(t):
        root_start(t + WINDOW)
        for p in range(2):
            i = t - LAG * (positions[p] - 1)
            passes = (positions[p] > 0) & (positions[p] < n_col - 1)
            for s in range(SECTIONS):
                c = i - s * PARTS

                @pl.when(passes & (c >= 0) & (c < PARTS))
                def _(p=p, s=s, c=c):
                    a_copy(p, s, c, False).wait_recv()
                    a_copy(p, s, c, False).start()

            if p == 0:

                @pl.when(passes & (i == 1))
                def _():
                    ma_copy().wait_recv()
                    ma_copy().start()

        i = t - LAG * (last_pair - 1 - pair)
        for s in range(SECTIONS):
            c = i - s * PARTS

            @pl.when(in_chain & (c >= 0) & (c < PARTS))
            def _(s=s, c=c):
                b_copy(s, c).wait_recv()

                @pl.when(pair > 0)
                def _():
                    b_copy(s, c).start()

                sib_copy(s, c).start()

            @pl.when(in_chain & (c == 1))
            def _(s=s):
                mb_copy(s, below * 2 + core, s).wait_recv()

                @pl.when(pair > 0)
                def _():
                    mb_copy(s, below * 2 + core, s).start()

    def section_ready(s):
        for p in range(2):

            @pl.when(positions[p] == n_col - 1)
            def _(p=p):
                for c in range(PARTS):
                    a_copy(p, s, c, False).wait_recv()

        @pl.when(is_left_root)
        def _():
            a_local(s).wait()

        @pl.when(in_chain)
        def _():
            for c in range(PARTS):
                sib_arrival(s, c).wait_recv()

        @pl.when(row == n_row - SECTIONS + s)
        def _():
            b_local(s).wait()

        @pl.when(row == n_row - 1 - s)
        def _():
            b_root_sibling(s).wait_recv()

    most = LAG * max(n_col - 3, last_pair - 1, 0)
    for t in range(PARTS + most):
        forward(t)

    @pl.when(positions[0] == n_col - 1)
    def _():
        ma_copy().wait_recv()

    for s in range(SECTIONS):

        @pl.when(row == n_row - 1 - s)
        def _(s=s):
            mb_copy(s, sibling, s).wait_recv()

    group = 4
    products = KA // group
    slots = PARTS // products

    def product(s, j):
        left = jnp.concatenate(
            [
                jnp.concatenate(
                    [lts[s][table_smem[s, 1, m * KA + j * group + a]] for a in range(group)],
                    axis=1,
                )
                for m in range(MB)
            ],
            axis=0,
        )
        right = jnp.concatenate(
            [
                jnp.concatenate(
                    [rts[s][table_smem[s, 0, (j * group + a) * NB + n]] for n in range(NB)], axis=1
                )
                for a in range(group)
            ],
            axis=0,
        )
        acc[...] += jnp.dot(left, right, preferred_element_type=jnp.float32)

    row_id = lax.broadcasted_iota(jnp.int32, (KB, TILE), 0)

    def make_table(s):
        table[0:1, :] = jnp.min(jnp.where(mb[s] == ma[s : s + 1, :], row_id, KB), axis=0, keepdims=True)
        table[1:2, :] = ma[SECTIONS + s : SECTIONS + s + 1, :]
        to_smem = pltpu.make_async_copy(table, table_smem.at[s], loc.at[4])
        to_smem.start()
        to_smem.wait()

    load_c.wait()
    for s in range(SECTIONS):
        section_ready(s)
        make_table(s)
        for j in range(products):
            if s + 1 < SECTIONS:
                for t in range(slots):
                    forward(PARTS + most + j * slots + t)
            product(s, j)

    partial = jnp.zeros((1, NB * TILE), jnp.float32)
    for m in range(MB):
        keep = jnp.concatenate(
            [
                jnp.full((1, TILE), mask_ref[m, n].astype(jnp.float32), jnp.float32)
                for n in range(NB)
            ],
            axis=1,
        )
        block = acc[m * TILE : (m + 1) * TILE, :]
        kept = block * block * keep
        acc[m * TILE : (m + 1) * TILE, :] = kept
        partial = partial + jnp.sum(kept, axis=0, keepdims=True)
    sums[row] = partial

    def cs_copy(target, slot):
        return pltpu.make_async_remote_copy(
            src_ref=sums.at[slot], dst_ref=sums.at[slot],
            send_sem=cs_send.at[target], recv_sem=cs_recv.at[slot],
            device_id=(target, col), device_id_type=MESH,
        )

    for d in range(1, n_row):
        cs_copy((row + d) % n_row, row).start()
    for d in range(1, n_row):
        source = (row + d) % n_row
        cs_copy(source, source).wait_recv()
    scale_ref[...] = total_rows / jnp.sum(sums[...], axis=0)

    for d in range(1, n_row):
        cs_copy((row + d) % n_row, row).wait_send()
    for p in range(2):

        @pl.when((positions[p] > 0) & (positions[p] < n_col - 1))
        def _(p=p):
            for i in range(steps):
                a_copy(p, i // PARTS, i % PARTS, False).wait_send()

        @pl.when(is_left_root)
        def _(p=p):
            for i in range(steps - WINDOW, steps):
                a_copy(p, i // PARTS, i % PARTS, True).wait_send()

    @pl.when(positions[0] < n_col - 1)
    def _():
        ma_copy().wait_send()

    @pl.when(in_chain)
    def _():
        for i in range(steps):
            sib_copy(i // PARTS, i % PARTS).wait_send()

        @pl.when(pair > 0)
        def _():
            for i in range(steps):
                b_copy(i // PARTS, i % PARTS).wait_send()
            for s in range(SECTIONS):
                mb_copy(s, below * 2 + core, s).wait_send()

    for s in range(SECTIONS):

        @pl.when(row == n_row - SECTIONS + s)
        def _(s=s):
            for k in range(2):
                mb_copy(s, below * 2 + k, k).wait_send()
            mb_copy(s, sibling, 2).wait_send()
            for c in range(PARTS - WINDOW, PARTS):
                for k in range(2):
                    b_root_copy(s, k, c).wait_send()
            b_root_sibling(s).wait_send()


def local(n_row, n_col, a_tiles, a_index, a_count, b_tiles, b_index, b_count, c_partial, prune_mask):
    hbm = pl.BlockSpec(memory_space=pltpu.HBM)
    steps = SECTIONS * PARTS
    dma = pltpu.SemaphoreType.DMA
    rows, columns = c_partial.shape
    kept, scale = pl.pallas_call(
        functools.partial(kernel, n_row, n_col),
        out_shape=(
            pltpu.VMEM((rows, columns), jnp.float32),
            pltpu.VMEM((1, columns), jnp.float32),
        ),
        in_specs=[hbm] * 8,
        out_specs=(pl.BlockSpec(memory_space=pltpu.VMEM), pl.BlockSpec(memory_space=pltpu.VMEM)),
        scratch_shapes=[
            pltpu.SMEM(a_index.shape, jnp.int32),
            pltpu.SMEM(a_count.shape, jnp.int32),
            pltpu.SMEM(b_index.shape, jnp.int32),
            pltpu.SMEM(b_count.shape, jnp.int32),
            pltpu.SMEM(prune_mask.shape, jnp.int32),
            pltpu.VMEM((KA + 1, TILE, TILE), jnp.bfloat16),
            pltpu.VMEM((KA + 1, TILE, TILE), jnp.bfloat16),
            pltpu.VMEM((KB + 1, TILE, TILE), jnp.bfloat16),
            pltpu.VMEM((KB + 1, TILE, TILE), jnp.bfloat16),
            pltpu.VMEM((2 * SECTIONS, TILE), jnp.int32),
            pltpu.VMEM((SECTIONS, KB, TILE), jnp.int32),
            pltpu.VMEM((2, TILE), jnp.int32),
            pltpu.SMEM((SECTIONS, 2, TILE), jnp.int32),
            pltpu.VMEM((n_row, 1, columns), jnp.float32),
            dma((2, steps)), dma((2, steps)),
            dma((steps,)), dma((steps,)), dma((steps,)), dma((steps,)),
            dma((1,)), dma((1,)), dma((3,)), dma((SECTIONS,)),
            dma((n_row,)), dma((n_row,)), dma((10,)),
        ],
        compiler_params=pltpu.CompilerParams(
            collective_id=0, has_side_effects=True, vmem_limit_bytes=60 * 1024 * 1024
        ),
        cost_estimate=pl.CostEstimate(
            flops=SECTIONS * 2 * rows * KA * TILE * columns, bytes_accessed=8 * rows * columns, transcendentals=0
        ),
    )(a_index, a_count, b_index, b_count, prune_mask, a_tiles, b_tiles, c_partial)
    return kept * scale


def solution(mesh):
    n_row, n_col = mesh.shape["row"], mesh.shape["col"]
    return jax.shard_map(
        functools.partial(local, n_row, n_col),
        mesh=mesh,
        in_specs=(
            P("row", "col", None, None, None, None),
            P("row", "col", None, None),
            P("row", "col", None),
            P("row", "col", None, None, None),
            P("row", "col", None),
            P("row", "col"),
            P("row", "col"),
            P("row", "col"),
        ),
        out_specs=P("row", "col"),
        check_vma=False,
    )
```

```python
import functools

import jax
import jax.numpy as jnp
from jax import lax
from jax.experimental import pallas as pl
from jax.experimental.pallas import tpu as pltpu
from jax.sharding import PartitionSpec as P

MB = 4
NB = 4
W = 32
KA = 16
KB = 16
SECTIONS = 2
TILE = 128
STEP = 2
PARTS = KA // 2 // STEP
WINDOW = 4
LAG = 2
MESH = pl.DeviceIdType.MESH


def grid_of(n_col):
    nx = max(d for d in range(1, n_col + 1) if n_col % d == 0 and d * d <= n_col)
    return n_col // nx, nx


def snake(index, outer, inner):
    o, i = index // inner, index % inner
    return o, (1 - o % 2) * i + (o % 2) * (inner - 1 - i)


def path_position(col, path, ny, nx):
    y, x = ny - 1 - col // nx, nx - 1 - col % nx
    if path == 0:
        return y * nx + (1 - y % 2) * x + (y % 2) * (nx - 1 - x)
    return x * ny + (1 - x % 2) * y + (x % 2) * (ny - 1 - y)


def path_column(position, path, ny, nx):
    if path == 0:
        y, x = snake(position, ny, nx)
    else:
        x, y = snake(position, nx, ny)
    return (ny - 1 - y) * nx + (nx - 1 - x)


def kernel(
    n_row, n_col, ai_hbm, ac_hbm, bi_hbm, bc_hbm, mask_hbm, a_hbm, b_hbm, c_hbm,
    acc, scale_ref,
    ai_ref, ac_ref, bi_ref, bc_ref, mask_ref, lt0, lt1, rt0, rt1, ma, mb, table, table_smem, sums,
    a_send, a_recv, b_send, b_recv, sib_send, sib_recv, ma_send, ma_recv, mb_send, mb_recv,
    cs_send, cs_recv, loc,
):
    row = lax.axis_index("row")
    col = lax.axis_index("col")
    pair, core = row // 2, row % 2
    last_pair = n_row // 2 - 1
    ny, nx = grid_of(n_col)
    lts, rts = (lt0, lt1), (rt0, rt1)
    total_rows = n_row * MB * TILE

    load_c = pltpu.make_async_copy(c_hbm, acc, loc.at[0])
    load_c.start()
    small = [
        pltpu.make_async_copy(source, target, loc.at[5 + i])
        for i, (source, target) in enumerate(
            ((ai_hbm, ai_ref), (ac_hbm, ac_ref), (bi_hbm, bi_ref), (bc_hbm, bc_ref), (mask_hbm, mask_ref))
        )
    ]
    for copy in small:
        copy.start()

    barrier = pltpu.get_barrier_semaphore()
    for d in range(1, n_row):
        pl.semaphore_signal(barrier, inc=1, device_id=((row + d) % n_row, col), device_id_type=MESH)
    for d in range(1, n_col):
        pl.semaphore_signal(barrier, inc=1, device_id=(row, (col + d) % n_col), device_id_type=MESH)

    for s in range(SECTIONS):
        lts[s][KA] = jnp.zeros((TILE, TILE), jnp.bfloat16)
        rts[s][KB] = jnp.zeros((TILE, TILE), jnp.bfloat16)

    pl.semaphore_wait(barrier, n_row - 1 + n_col - 1)

    positions = [path_position(col, p, ny, nx) for p in range(2)]
    is_left_root = col == n_col - 1

    def next_col(p):
        return path_column((positions[p] + 1) % n_col, p, ny, nx)

    def a_copy(p, s, c, from_hbm):
        i = s * PARTS + c
        tiles = pl.ds(p * (KA // 2) + c * STEP, STEP)
        return pltpu.make_async_remote_copy(
            src_ref=a_hbm.at[0, 0, s, tiles] if from_hbm else lts[s].at[tiles],
            dst_ref=lts[s].at[tiles],
            send_sem=a_send.at[p, i], recv_sem=a_recv.at[p, i],
            device_id=(row, next_col(p)), device_id_type=MESH,
        )

    def ma_copy():
        return pltpu.make_async_remote_copy(
            src_ref=ma, dst_ref=ma, send_sem=ma_send.at[0], recv_sem=ma_recv.at[0],
            device_id=(row, next_col(0)), device_id_type=MESH,
        )

    def a_local(s):
        return pltpu.make_async_copy(a_hbm.at[0, 0, s], lts[s].at[pl.ds(0, KA)], loc.at[1 + s])

    below = (pair - 1 + last_pair + 1) % (last_pair + 1)
    sibling = pair * 2 + 1 - core

    def b_root_copy(s, k, c):
        tiles = pl.ds(k * (KB // 2) + c * STEP, STEP)
        return pltpu.make_async_remote_copy(
            src_ref=b_hbm.at[0, 0, tiles], dst_ref=rts[s].at[tiles],
            send_sem=b_send.at[k * PARTS + c], recv_sem=b_recv.at[s * PARTS + c],
            device_id=(below * 2 + k, col), device_id_type=MESH,
        )

    def b_root_sibling(s):
        return pltpu.make_async_remote_copy(
            src_ref=b_hbm.at[0, 0], dst_ref=rts[s].at[pl.ds(0, KB)],
            send_sem=sib_send.at[0], recv_sem=sib_recv.at[s * PARTS],
            device_id=(sibling, col), device_id_type=MESH,
        )

    def mb_copy(s, target, sem):
        return pltpu.make_async_remote_copy(
            src_ref=mb.at[s], dst_ref=mb.at[s], send_sem=mb_send.at[sem], recv_sem=mb_recv.at[s],
            device_id=(target, col), device_id_type=MESH,
        )

    def b_chain_copy(s, c, k, target, send, recv):
        ref = rts[s].at[pl.ds(k * (KB // 2) + c * STEP, STEP)]
        i = s * PARTS + c
        return pltpu.make_async_remote_copy(
            src_ref=ref, dst_ref=ref, send_sem=send.at[i], recv_sem=recv.at[i],
            device_id=(target, col), device_id_type=MESH,
        )

    def b_copy(s, c):
        return b_chain_copy(s, c, core, below * 2 + core, b_send, b_recv)

    def sib_copy(s, c):
        return b_chain_copy(s, c, core, sibling, sib_send, sib_recv)

    def sib_arrival(s, c):
        return b_chain_copy(s, c, 1 - core, sibling, sib_send, sib_recv)

    def b_local(s):
        return pltpu.make_async_copy(b_hbm.at[0, 0], rts[s].at[pl.ds(0, KB)], loc.at[3])

    steps = SECTIONS * PARTS
    in_chain = pair < last_pair

    def root_start(t):
        if t < steps:

            @pl.when(is_left_root)
            def _():
                for p in range(2):
                    if t >= WINDOW:
                        a_copy(p, (t - WINDOW) // PARTS, (t - WINDOW) % PARTS, True).wait_send()
                    a_copy(p, t // PARTS, t % PARTS, True).start()

        for s in range(SECTIONS):
            c = t - PARTS * s
            if 0 <= c < PARTS:

                @pl.when(row == n_row - SECTIONS + s)
                def _(s=s, c=c):
                    for k in range(2):
                        if c >= WINDOW:
                            b_root_copy(s, k, c - WINDOW).wait_send()
                        b_root_copy(s, k, c).start()

    for t in range(WINDOW):
        root_start(t)

    @pl.when(is_left_root)
    def _():
        for s in range(SECTIONS):
            a_local(s).start()

    for s in range(SECTIONS):

        @pl.when(row == n_row - SECTIONS + s)
        def _(s=s):
            b_root_sibling(s).start()
            b_local(s).start()

    for copy in small:
        copy.wait()
    lane = lax.broadcasted_iota(jnp.int32, (1, TILE), 1)

    @pl.when(col == n_col - 1)
    def _():
        for s in range(SECTIONS):
            count = ac_ref[0, 0, s]
            target = jnp.full((1, TILE), -2, jnp.int32)
            place = jnp.full((1, TILE), KA, jnp.int32)
            for a in range(KA):
                slot = ai_ref[0, 0, s, a]
                live = a < count
                inner = jnp.where(live, (slot % W) * NB, -64)
                block = jnp.where(live, slot // W, -1)
                target = jnp.where(lane // NB == a, inner + lane % NB, target)
                place = jnp.where(lane == block * KA + a, jnp.where(live, a, KA), place)
            ma[s : s + 1, :] = target
            ma[SECTIONS + s : SECTIONS + s + 1, :] = place

    for s in range(SECTIONS):

        @pl.when(row == n_row - SECTIONS + s)
        def _(s=s):
            count = bc_ref[0, 0]
            for b in range(KB):
                slot = jnp.where(b < count, bi_ref[0, 0, b], -1)
                mb[s, b : b + 1, :] = jnp.full((1, TILE), slot, jnp.int32)

    @pl.when(is_left_root)
    def _():
        ma_copy().start()

    for s in range(SECTIONS):

        @pl.when(row == n_row - SECTIONS + s)
        def _(s=s):
            for k in range(2):
                mb_copy(s, below * 2 + k, k).start()
            mb_copy(s, sibling, 2).start()

    def forward(t):
        root_start(t + WINDOW)
        for p in range(2):
            i = t - LAG * (positions[p] - 1)
            passes = (positions[p] > 0) & (positions[p] < n_col - 1)
            for s in range(SECTIONS):
                c = i - s * PARTS

                @pl.when(passes & (c >= 0) & (c < PARTS))
                def _(p=p, s=s, c=c):
                    a_copy(p, s, c, False).wait_recv()
                    a_copy(p, s, c, False).start()

            if p == 0:

                @pl.when(passes & (i == 1))
                def _():
                    ma_copy().wait_recv()
                    ma_copy().start()

        i = t - LAG * (last_pair - 1 - pair)
        for s in range(SECTIONS):
            c = i - s * PARTS

            @pl.when(in_chain & (c >= 0) & (c < PARTS))
            def _(s=s, c=c):
                b_copy(s, c).wait_recv()

                @pl.when(pair > 0)
                def _():
                    b_copy(s, c).start()

                sib_copy(s, c).start()

            @pl.when(in_chain & (c == 1))
            def _(s=s):
                mb_copy(s, below * 2 + core, s).wait_recv()

                @pl.when(pair > 0)
                def _():
                    mb_copy(s, below * 2 + core, s).start()

    def section_ready(s):
        for p in range(2):

            @pl.when(positions[p] == n_col - 1)
            def _(p=p):
                for c in range(PARTS):
                    a_copy(p, s, c, False).wait_recv()

        @pl.when(is_left_root)
        def _():
            a_local(s).wait()

        @pl.when(in_chain)
        def _():
            for c in range(PARTS):
                sib_arrival(s, c).wait_recv()

        @pl.when(row == n_row - SECTIONS + s)
        def _():
            b_local(s).wait()

        @pl.when(row == n_row - 1 - s)
        def _():
            b_root_sibling(s).wait_recv()

    most = LAG * max(n_col - 3, last_pair - 1, 0)
    for t in range(PARTS + most):
        forward(t)

    @pl.when(positions[0] == n_col - 1)
    def _():
        ma_copy().wait_recv()

    for s in range(SECTIONS):
        @pl.when(row == n_row - 1 - s)
        def _(s=s):
            mb_copy(s, sibling, s).wait_recv()

    group = KA // PARTS

    def product(s, j):
        left = jnp.concatenate(
            [
                jnp.concatenate(
                    [lts[s][table_smem[s, 1, m * KA + j * group + a]] for a in range(group)],
                    axis=1,
                )
                for m in range(MB)
            ],
            axis=0,
        )
        right = jnp.concatenate(
            [
                jnp.concatenate(
                    [rts[s][table_smem[s, 0, (j * group + a) * NB + n]] for n in range(NB)], axis=1
                )
                for a in range(group)
            ],
            axis=0,
        )
        acc[...] += jnp.dot(left, right, preferred_element_type=jnp.float32)

    row_id = lax.broadcasted_iota(jnp.int32, (KB, TILE), 0)

    def make_table(s):
        table[0:1, :] = jnp.min(jnp.where(mb[s] == ma[s : s + 1, :], row_id, KB), axis=0, keepdims=True)
        table[1:2, :] = ma[SECTIONS + s : SECTIONS + s + 1, :]
        to_smem = pltpu.make_async_copy(table, table_smem.at[s], loc.at[4])
        to_smem.start()
        to_smem.wait()

    load_c.wait()
    for s in range(SECTIONS):
        section_ready(s)
        make_table(s)
        for j in range(PARTS):
            if s + 1 < SECTIONS:
                forward(PARTS + most + j)
            product(s, j)

    partial = jnp.zeros((1, NB * TILE), jnp.float32)
    for m in range(MB):
        keep = jnp.concatenate(
            [
                jnp.full((1, TILE), mask_ref[m, n].astype(jnp.float32), jnp.float32)
                for n in range(NB)
            ],
            axis=1,
        )
        block = acc[m * TILE : (m + 1) * TILE, :]
        kept = block * block * keep
        acc[m * TILE : (m + 1) * TILE, :] = kept
        partial = partial + jnp.sum(kept, axis=0, keepdims=True)
    sums[row] = partial

    def cs_copy(target, slot):
        return pltpu.make_async_remote_copy(
            src_ref=sums.at[slot], dst_ref=sums.at[slot],
            send_sem=cs_send.at[target], recv_sem=cs_recv.at[slot],
            device_id=(target, col), device_id_type=MESH,
        )

    for d in range(1, n_row):
        cs_copy((row + d) % n_row, row).start()
    for d in range(1, n_row):
        source = (row + d) % n_row
        cs_copy(source, source).wait_recv()
    scale_ref[...] = total_rows / jnp.sum(sums[...], axis=0)

    for d in range(1, n_row):
        cs_copy((row + d) % n_row, row).wait_send()
    for p in range(2):

        @pl.when((positions[p] > 0) & (positions[p] < n_col - 1))
        def _(p=p):
            for i in range(steps):
                a_copy(p, i // PARTS, i % PARTS, False).wait_send()

        @pl.when(is_left_root)
        def _(p=p):
            for i in range(steps - WINDOW, steps):
                a_copy(p, i // PARTS, i % PARTS, True).wait_send()

    @pl.when(positions[0] < n_col - 1)
    def _():
        ma_copy().wait_send()

    @pl.when(in_chain)
    def _():
        for i in range(steps):
            sib_copy(i // PARTS, i % PARTS).wait_send()

        @pl.when(pair > 0)
        def _():
            for i in range(steps):
                b_copy(i // PARTS, i % PARTS).wait_send()
            for s in range(SECTIONS):
                mb_copy(s, below * 2 + core, s).wait_send()

    for s in range(SECTIONS):

        @pl.when(row == n_row - SECTIONS + s)
        def _(s=s):
            for k in range(2):
                mb_copy(s, below * 2 + k, k).wait_send()
            mb_copy(s, sibling, 2).wait_send()
            for c in range(PARTS - WINDOW, PARTS):
                for k in range(2):
                    b_root_copy(s, k, c).wait_send()
            b_root_sibling(s).wait_send()


def local(n_row, n_col, a_tiles, a_index, a_count, b_tiles, b_index, b_count, c_partial, prune_mask):
    hbm = pl.BlockSpec(memory_space=pltpu.HBM)
    steps = SECTIONS * PARTS
    dma = pltpu.SemaphoreType.DMA
    rows, columns = c_partial.shape
    kept, scale = pl.pallas_call(
        functools.partial(kernel, n_row, n_col),
        out_shape=(
            pltpu.VMEM((rows, columns), jnp.float32),
            pltpu.VMEM((1, columns), jnp.float32),
        ),
        in_specs=[hbm] * 8,
        out_specs=(pl.BlockSpec(memory_space=pltpu.VMEM), pl.BlockSpec(memory_space=pltpu.VMEM)),
        scratch_shapes=[
            pltpu.SMEM(a_index.shape, jnp.int32),
            pltpu.SMEM(a_count.shape, jnp.int32),
            pltpu.SMEM(b_index.shape, jnp.int32),
            pltpu.SMEM(b_count.shape, jnp.int32),
            pltpu.SMEM(prune_mask.shape, jnp.int32),
            pltpu.VMEM((KA + 1, TILE, TILE), jnp.bfloat16),
            pltpu.VMEM((KA + 1, TILE, TILE), jnp.bfloat16),
            pltpu.VMEM((KB + 1, TILE, TILE), jnp.bfloat16),
            pltpu.VMEM((KB + 1, TILE, TILE), jnp.bfloat16),
            pltpu.VMEM((2 * SECTIONS, TILE), jnp.int32),
            pltpu.VMEM((SECTIONS, KB, TILE), jnp.int32),
            pltpu.VMEM((2, TILE), jnp.int32),
            pltpu.SMEM((SECTIONS, 2, TILE), jnp.int32),
            pltpu.VMEM((n_row, 1, columns), jnp.float32),
            dma((2, steps)), dma((2, steps)),
            dma((steps,)), dma((steps,)), dma((steps,)), dma((steps,)),
            dma((1,)), dma((1,)), dma((3,)), dma((SECTIONS,)),
            dma((n_row,)), dma((n_row,)), dma((10,)),
        ],
        compiler_params=pltpu.CompilerParams(
            collective_id=0, has_side_effects=True, vmem_limit_bytes=60 * 1024 * 1024
        ),
        cost_estimate=pl.CostEstimate(
            flops=SECTIONS * 2 * rows * KA * TILE * columns, bytes_accessed=8 * rows * columns, transcendentals=0
        ),
    )(a_index, a_count, b_index, b_count, prune_mask, a_tiles, b_tiles, c_partial)
    return kept * scale


def solution(mesh):
    n_row, n_col = mesh.shape["row"], mesh.shape["col"]
    return jax.shard_map(
        functools.partial(local, n_row, n_col),
        mesh=mesh,
        in_specs=(
            P("row", "col", None, None, None, None),
            P("row", "col", None, None),
            P("row", "col", None),
            P("row", "col", None, None, None),
            P("row", "col", None),
            P("row", "col"),
            P("row", "col"),
            P("row", "col"),
        ),
        out_specs=P("row", "col"),
        check_vma=False,
    )
```

```python
import functools

import jax
import jax.numpy as jnp
from jax import lax
from jax.experimental import pallas as pl
from jax.experimental.pallas import tpu as pltpu
from jax.sharding import PartitionSpec as P

MB = 4
NB = 4
W = 32
KA = 16
KB = 16
SECTIONS = 2
TILE = 128
STEP = 2
PARTS = KA // 2 // STEP
WINDOW = 2
LAG = 2
AHEAD = 2
MESH = pl.DeviceIdType.MESH


def grid_of(n_col):
    nx = max(d for d in range(1, n_col + 1) if n_col % d == 0 and d * d <= n_col)
    return n_col // nx, nx


def snake(index, outer, inner):
    o, i = index // inner, index % inner
    return o, (1 - o % 2) * i + (o % 2) * (inner - 1 - i)


def path_position(col, path, ny, nx):
    y, x = ny - 1 - col // nx, nx - 1 - col % nx
    if path == 0:
        return y * nx + (1 - y % 2) * x + (y % 2) * (nx - 1 - x)
    return x * ny + (1 - x % 2) * y + (x % 2) * (ny - 1 - y)


def path_column(position, path, ny, nx):
    if path == 0:
        y, x = snake(position, ny, nx)
    else:
        x, y = snake(position, nx, ny)
    return (ny - 1 - y) * nx + (nx - 1 - x)


def kernel(
    n_row, n_col, ai_hbm, ac_hbm, bi_hbm, bc_hbm, mask_hbm, a_hbm, b_hbm, c_hbm,
    acc, scale_ref,
    ai_ref, ac_ref, bi_ref, bc_ref, mask_ref, lt0, lt1, rt0, rt1, ma, mb, table, table_smem, sums,
    a_send, a_recv, b_send, b_recv, sib_send, sib_recv, ma_send, ma_recv, mb_send, mb_recv,
    cs_send, cs_recv, loc,
):
    row = lax.axis_index("row")
    col = lax.axis_index("col")
    pair, core = row // 2, row % 2
    last_pair = n_row // 2 - 1
    ny, nx = grid_of(n_col)
    lts, rts = (lt0, lt1), (rt0, rt1)
    total_rows = n_row * MB * TILE

    load_c = pltpu.make_async_copy(c_hbm, acc, loc.at[0])
    load_c.start()
    small = [
        pltpu.make_async_copy(source, target, loc.at[5 + i])
        for i, (source, target) in enumerate(
            ((ai_hbm, ai_ref), (ac_hbm, ac_ref), (bi_hbm, bi_ref), (bc_hbm, bc_ref), (mask_hbm, mask_ref))
        )
    ]
    for copy in small:
        copy.start()

    barrier = pltpu.get_barrier_semaphore()
    for d in range(1, n_row):
        pl.semaphore_signal(barrier, inc=1, device_id=((row + d) % n_row, col), device_id_type=MESH)
    for d in range(1, n_col):
        pl.semaphore_signal(barrier, inc=1, device_id=(row, (col + d) % n_col), device_id_type=MESH)

    for s in range(SECTIONS):
        lts[s][KA] = jnp.zeros((TILE, TILE), jnp.bfloat16)
        rts[s][KB] = jnp.zeros((TILE, TILE), jnp.bfloat16)

    pl.semaphore_wait(barrier, n_row - 1 + n_col - 1)

    positions = [path_position(col, p, ny, nx) for p in range(2)]
    is_left_root = col == n_col - 1

    def next_col(p):
        return path_column((positions[p] + 1) % n_col, p, ny, nx)

    def a_copy(p, s, c, from_hbm):
        i = s * PARTS + c
        tiles = pl.ds(p * (KA // 2) + c * STEP, STEP)
        return pltpu.make_async_remote_copy(
            src_ref=a_hbm.at[0, 0, s, tiles] if from_hbm else lts[s].at[tiles],
            dst_ref=lts[s].at[tiles],
            send_sem=a_send.at[p, i], recv_sem=a_recv.at[p, i],
            device_id=(row, next_col(p)), device_id_type=MESH,
        )

    def ma_copy():
        return pltpu.make_async_remote_copy(
            src_ref=ma, dst_ref=ma, send_sem=ma_send.at[0], recv_sem=ma_recv.at[0],
            device_id=(row, next_col(0)), device_id_type=MESH,
        )

    def a_local(s):
        return pltpu.make_async_copy(a_hbm.at[0, 0, s], lts[s].at[pl.ds(0, KA)], loc.at[1 + s])

    below = (pair - 1 + last_pair + 1) % (last_pair + 1)
    sibling = pair * 2 + 1 - core

    def b_root_copy(s, k, c):
        tiles = pl.ds(k * (KB // 2) + c * STEP, STEP)
        return pltpu.make_async_remote_copy(
            src_ref=b_hbm.at[0, 0, tiles], dst_ref=rts[s].at[tiles],
            send_sem=b_send.at[k * PARTS + c], recv_sem=b_recv.at[s * PARTS + c],
            device_id=(below * 2 + k, col), device_id_type=MESH,
        )

    def b_root_sibling(s):
        return pltpu.make_async_remote_copy(
            src_ref=b_hbm.at[0, 0], dst_ref=rts[s].at[pl.ds(0, KB)],
            send_sem=sib_send.at[0], recv_sem=sib_recv.at[s * PARTS],
            device_id=(sibling, col), device_id_type=MESH,
        )

    def mb_copy(s, target, sem):
        return pltpu.make_async_remote_copy(
            src_ref=mb.at[s], dst_ref=mb.at[s], send_sem=mb_send.at[sem], recv_sem=mb_recv.at[s],
            device_id=(target, col), device_id_type=MESH,
        )

    def b_chain_copy(s, c, k, target, send, recv):
        ref = rts[s].at[pl.ds(k * (KB // 2) + c * STEP, STEP)]
        i = s * PARTS + c
        return pltpu.make_async_remote_copy(
            src_ref=ref, dst_ref=ref, send_sem=send.at[i], recv_sem=recv.at[i],
            device_id=(target, col), device_id_type=MESH,
        )

    def b_copy(s, c):
        return b_chain_copy(s, c, core, below * 2 + core, b_send, b_recv)

    def sib_copy(s, c):
        return b_chain_copy(s, c, core, sibling, sib_send, sib_recv)

    def sib_arrival(s, c):
        return b_chain_copy(s, c, 1 - core, sibling, sib_send, sib_recv)

    def b_local(s):
        return pltpu.make_async_copy(b_hbm.at[0, 0], rts[s].at[pl.ds(0, KB)], loc.at[3])

    steps = SECTIONS * PARTS
    in_chain = pair < last_pair

    def root_start(t):
        if t < steps:

            @pl.when(is_left_root)
            def _():
                for p in range(2):
                    if t >= WINDOW:
                        a_copy(p, (t - WINDOW) // PARTS, (t - WINDOW) % PARTS, True).wait_send()
                    a_copy(p, t // PARTS, t % PARTS, True).start()

        for s in range(SECTIONS):
            c = t - WINDOW * s
            if 0 <= c < PARTS:

                @pl.when(row == n_row - SECTIONS + s)
                def _(s=s, c=c):
                    for k in range(2):
                        if c >= WINDOW:
                            b_root_copy(s, k, c - WINDOW).wait_send()
                        b_root_copy(s, k, c).start()

    for t in range(WINDOW):
        root_start(t)

    @pl.when(is_left_root)
    def _():
        for s in range(SECTIONS):
            a_local(s).start()

    for s in range(SECTIONS):

        @pl.when(row == n_row - SECTIONS + s)
        def _(s=s):
            b_root_sibling(s).start()
            b_local(s).start()

    for copy in small:
        copy.wait()
    lane = lax.broadcasted_iota(jnp.int32, (1, TILE), 1)

    @pl.when(col == n_col - 1)
    def _():
        for s in range(SECTIONS):
            count = ac_ref[0, 0, s]
            target = jnp.full((1, TILE), -2, jnp.int32)
            place = jnp.full((1, TILE), KA, jnp.int32)
            for a in range(KA):
                slot = ai_ref[0, 0, s, a]
                live = a < count
                inner = jnp.where(live, (slot % W) * NB, -64)
                block = jnp.where(live, slot // W, -1)
                target = jnp.where(lane // NB == a, inner + lane % NB, target)
                place = jnp.where(lane == block * KA + a, jnp.where(live, a, KA), place)
            ma[s : s + 1, :] = target
            ma[SECTIONS + s : SECTIONS + s + 1, :] = place

    for s in range(SECTIONS):

        @pl.when(row == n_row - SECTIONS + s)
        def _(s=s):
            count = bc_ref[0, 0]
            for b in range(KB):
                slot = jnp.where(b < count, bi_ref[0, 0, b], -1)
                mb[s, b : b + 1, :] = jnp.full((1, TILE), slot, jnp.int32)

    @pl.when(is_left_root)
    def _():
        ma_copy().start()

    for s in range(SECTIONS):

        @pl.when(row == n_row - SECTIONS + s)
        def _(s=s):
            for k in range(2):
                mb_copy(s, below * 2 + k, k).start()
            mb_copy(s, sibling, 2).start()

    def forward(t):
        root_start(t + WINDOW)
        for p in range(2):
            i = t - LAG * (positions[p] - 1)
            passes = (positions[p] > 0) & (positions[p] < n_col - 1)
            for s in range(SECTIONS):
                c = i - s * PARTS

                @pl.when(passes & (c >= 0) & (c < PARTS))
                def _(p=p, s=s, c=c):
                    a_copy(p, s, c, False).wait_recv()
                    a_copy(p, s, c, False).start()

            if p == 0:

                @pl.when(passes & (i == 1))
                def _():
                    ma_copy().wait_recv()
                    ma_copy().start()

        i = t - LAG * (last_pair - 1 - pair)
        for s in range(SECTIONS):
            c = i - s * PARTS

            @pl.when(in_chain & (c >= 0) & (c < PARTS))
            def _(s=s, c=c):
                b_copy(s, c).wait_recv()

                @pl.when(pair > 0)
                def _():
                    b_copy(s, c).start()

                sib_copy(s, c).start()

            @pl.when(in_chain & (c == 1))
            def _(s=s):
                mb_copy(s, below * 2 + core, s).wait_recv()

                @pl.when(pair > 0)
                def _():
                    mb_copy(s, below * 2 + core, s).start()

    def section_ready(s):
        for p in range(2):

            @pl.when(positions[p] == n_col - 1)
            def _(p=p):
                for c in range(PARTS):
                    a_copy(p, s, c, False).wait_recv()

        @pl.when(is_left_root)
        def _():
            a_local(s).wait()

        @pl.when(in_chain)
        def _():
            for c in range(PARTS):
                sib_arrival(s, c).wait_recv()

        @pl.when(row == n_row - SECTIONS + s)
        def _():
            b_local(s).wait()

        @pl.when(row == n_row - 1 - s)
        def _():
            b_root_sibling(s).wait_recv()

    most = LAG * max(n_col - 3, last_pair - 1, 0)
    for t in range(PARTS + most + AHEAD):
        forward(t)

    @pl.when(positions[0] == n_col - 1)
    def _():
        ma_copy().wait_recv()

    for s in range(SECTIONS):
        @pl.when(row == n_row - 1 - s)
        def _(s=s):
            mb_copy(s, sibling, s).wait_recv()

    group = KA // PARTS

    def product(s, j):
        left = jnp.concatenate(
            [
                jnp.concatenate(
                    [lts[s][table_smem[s, 1, m * KA + j * group + a]] for a in range(group)],
                    axis=1,
                )
                for m in range(MB)
            ],
            axis=0,
        )
        right = jnp.concatenate(
            [
                jnp.concatenate(
                    [rts[s][table_smem[s, 0, (j * group + a) * NB + n]] for n in range(NB)], axis=1
                )
                for a in range(group)
            ],
            axis=0,
        )
        acc[...] += jnp.dot(left, right, preferred_element_type=jnp.float32)

    row_id = lax.broadcasted_iota(jnp.int32, (KB, TILE), 0)

    def make_table(s):
        table[0:1, :] = jnp.min(jnp.where(mb[s] == ma[s : s + 1, :], row_id, KB), axis=0, keepdims=True)
        table[1:2, :] = ma[SECTIONS + s : SECTIONS + s + 1, :]
        to_smem = pltpu.make_async_copy(table, table_smem.at[s], loc.at[4])
        to_smem.start()
        to_smem.wait()

    load_c.wait()
    for s in range(SECTIONS):
        section_ready(s)
        make_table(s)
        for j in range(PARTS):
            if s + 1 < SECTIONS and j < PARTS - AHEAD:
                forward(PARTS + most + AHEAD + j)
            product(s, j)

    partial = jnp.zeros((1, NB * TILE), jnp.float32)
    for m in range(MB):
        keep = jnp.concatenate(
            [
                jnp.full((1, TILE), mask_ref[m, n].astype(jnp.float32), jnp.float32)
                for n in range(NB)
            ],
            axis=1,
        )
        block = acc[m * TILE : (m + 1) * TILE, :]
        kept = block * block * keep
        acc[m * TILE : (m + 1) * TILE, :] = kept
        partial = partial + jnp.sum(kept, axis=0, keepdims=True)
    sums[row] = partial

    def cs_copy(target, slot):
        return pltpu.make_async_remote_copy(
            src_ref=sums.at[slot], dst_ref=sums.at[slot],
            send_sem=cs_send.at[target], recv_sem=cs_recv.at[slot],
            device_id=(target, col), device_id_type=MESH,
        )

    for d in range(1, n_row):
        cs_copy((row + d) % n_row, row).start()
    for d in range(1, n_row):
        source = (row + d) % n_row
        cs_copy(source, source).wait_recv()
    scale_ref[...] = total_rows / jnp.sum(sums[...], axis=0)

    for d in range(1, n_row):
        cs_copy((row + d) % n_row, row).wait_send()
    for p in range(2):

        @pl.when((positions[p] > 0) & (positions[p] < n_col - 1))
        def _(p=p):
            for i in range(steps):
                a_copy(p, i // PARTS, i % PARTS, False).wait_send()

        @pl.when(is_left_root)
        def _(p=p):
            for i in range(steps - WINDOW, steps):
                a_copy(p, i // PARTS, i % PARTS, True).wait_send()

    @pl.when(positions[0] < n_col - 1)
    def _():
        ma_copy().wait_send()

    @pl.when(in_chain)
    def _():
        for i in range(steps):
            sib_copy(i // PARTS, i % PARTS).wait_send()

        @pl.when(pair > 0)
        def _():
            for i in range(steps):
                b_copy(i // PARTS, i % PARTS).wait_send()
            for s in range(SECTIONS):
                mb_copy(s, below * 2 + core, s).wait_send()

    for s in range(SECTIONS):

        @pl.when(row == n_row - SECTIONS + s)
        def _(s=s):
            for k in range(2):
                mb_copy(s, below * 2 + k, k).wait_send()
            mb_copy(s, sibling, 2).wait_send()
            for c in range(PARTS - WINDOW, PARTS):
                for k in range(2):
                    b_root_copy(s, k, c).wait_send()
            b_root_sibling(s).wait_send()


def local(n_row, n_col, a_tiles, a_index, a_count, b_tiles, b_index, b_count, c_partial, prune_mask):
    hbm = pl.BlockSpec(memory_space=pltpu.HBM)
    steps = SECTIONS * PARTS
    dma = pltpu.SemaphoreType.DMA
    rows, columns = c_partial.shape
    kept, scale = pl.pallas_call(
        functools.partial(kernel, n_row, n_col),
        out_shape=(
            pltpu.VMEM((rows, columns), jnp.float32),
            pltpu.VMEM((1, columns), jnp.float32),
        ),
        in_specs=[hbm] * 8,
        out_specs=(pl.BlockSpec(memory_space=pltpu.VMEM), pl.BlockSpec(memory_space=pltpu.VMEM)),
        scratch_shapes=[
            pltpu.SMEM(a_index.shape, jnp.int32),
            pltpu.SMEM(a_count.shape, jnp.int32),
            pltpu.SMEM(b_index.shape, jnp.int32),
            pltpu.SMEM(b_count.shape, jnp.int32),
            pltpu.SMEM(prune_mask.shape, jnp.int32),
            pltpu.VMEM((KA + 1, TILE, TILE), jnp.bfloat16),
            pltpu.VMEM((KA + 1, TILE, TILE), jnp.bfloat16),
            pltpu.VMEM((KB + 1, TILE, TILE), jnp.bfloat16),
            pltpu.VMEM((KB + 1, TILE, TILE), jnp.bfloat16),
            pltpu.VMEM((2 * SECTIONS, TILE), jnp.int32),
            pltpu.VMEM((SECTIONS, KB, TILE), jnp.int32),
            pltpu.VMEM((2, TILE), jnp.int32),
            pltpu.SMEM((SECTIONS, 2, TILE), jnp.int32),
            pltpu.VMEM((n_row, 1, columns), jnp.float32),
            dma((2, steps)), dma((2, steps)),
            dma((steps,)), dma((steps,)), dma((steps,)), dma((steps,)),
            dma((1,)), dma((1,)), dma((3,)), dma((SECTIONS,)),
            dma((n_row,)), dma((n_row,)), dma((10,)),
        ],
        compiler_params=pltpu.CompilerParams(
            collective_id=0, has_side_effects=True, vmem_limit_bytes=60 * 1024 * 1024
        ),
        cost_estimate=pl.CostEstimate(
            flops=SECTIONS * 2 * rows * KA * TILE * columns, bytes_accessed=8 * rows * columns, transcendentals=0
        ),
    )(a_index, a_count, b_index, b_count, prune_mask, a_tiles, b_tiles, c_partial)
    return kept * scale


def solution(mesh):
    n_row, n_col = mesh.shape["row"], mesh.shape["col"]
    return jax.shard_map(
        functools.partial(local, n_row, n_col),
        mesh=mesh,
        in_specs=(
            P("row", "col", None, None, None, None),
            P("row", "col", None, None),
            P("row", "col", None),
            P("row", "col", None, None, None),
            P("row", "col", None),
            P("row", "col"),
            P("row", "col"),
            P("row", "col"),
        ),
        out_specs=P("row", "col"),
        check_vma=False,
    )
```
